256 devices in a mesh: dp: 16 (over x_lo, z), mp: 16 (over x_hi, y, core).
Axes of the slice: x: 4 (x_hi: 2, x_lo: 2; x = x_hi * 2 + x_lo), y: 4, z: 8, core: 2. Of those that a mesh axis runs over, the one named last changes fastest.
Arguments:
- tokens: bfloat16 [8192, 6144], P('dp', 'mp'), may hold values from -120 to 120
- w_qkv: bfloat16 [6144, 3, 4096], P(None, None, 'mp'), may hold values from -0.078125 to 0.078125
- cotangent: bfloat16 [8192, 4096], P('dp', 'mp'), may hold values from -6 to 6
Outputs:
- attended: bfloat16 [8192, 4096], P('dp', 'mp')
- grad_tokens: bfloat16 [8192, 6144], P('dp', 'mp')
- grad_w: bfloat16 [6144, 3, 4096], P('dp', None, 'mp')
The draws below stay inside these ranges and needn't reach their ends.
All inputs are finite; a program needn't handle non-finite values.
Results may differ from the reference program's by a relative error of at most 0.025.
Values may be sent and summed in bfloat16 or wider, within the bound.
No kernel may reach another device: no remote copies, remote signals or barrier semaphores. Data moves between devices by JAX's collectives and lax.ppermute only.
A program may use at most 192 MiB of HBM per device.

```python
import math
import jax
import jax.numpy as jnp
from jax import lax

D = 6144
HEAD_DIM = 128
PATCHES = 256
HEADS = 32
TOK_DEV = 512
TOKENS = 8192
N_DP = 16


def draw_tokens(key, part):
    key = jax.random.fold_in(key, 11)
    k_rows, k_cols, k_base = jax.random.split(key, 3)
    row_scale = jnp.exp(jax.random.uniform(k_rows, (TOKENS, 1), jnp.float32, 0.0, math.log(10.0)))
    col_scale = jnp.exp(jax.random.uniform(k_cols, (1, D), jnp.float32, math.log(0.3), math.log(3.0)))
    base_draw = jax.random.truncated_normal(k_base, -4.0, 4.0, (TOKENS, D), jnp.float32)
    return (base_draw * row_scale * col_scale).astype(jnp.bfloat16)


def level_of(own_key, shape, pieces, low, high):
    level, own = 1.0, jax.random.fold_in(own_key, 6)
    for position, shards_of in pieces:
        draws = jnp.exp(jax.random.uniform(jax.random.fold_in(own, position), (shards_of,), jnp.float32, low / len(pieces), high / len(pieces)))
        level = level * jnp.repeat(draws, shape[position] // shards_of).reshape([-1 if axis == position else 1 for axis in range(len(shape))])
    return level


def gaussian(stream_key, extent, spread, reach, cuts=(), held_as=jnp.bfloat16):
    array = jax.random.normal(stream_key, extent, jnp.float32) * spread
    if len(cuts) > 0:
        array = level_of(stream_key, extent, cuts, -0.22, 0.18) * array
    return jnp.clip(array, min=-reach, max=reach).astype(held_as)


def setup_inputs(seed: int = 0) -> dict:
    key_list = jax.random.split(jax.random.key(seed), 4)
    tokens = draw_tokens(jax.random.fold_in(key_list[3], 71), 0)
    w_qkv = gaussian(key_list[1], (D, 3, HEADS * HEAD_DIM), D ** -0.5, 0.078125, ((2, 16),))
    cotangent = gaussian(key_list[2], (TOKENS, HEADS * HEAD_DIM), 1.0, 6.0, ((0, 16), (1, 16)))
    return {"tokens": tokens, "w_qkv": w_qkv, "cotangent": cotangent}


EPS = 1e-06

def row_norm(values):
    row_mean = lax.optimization_barrier(jnp.mean(values, axis=-1, keepdims=True))
    centred = values - row_mean
    variance = lax.optimization_barrier(jnp.mean(centred * centred, axis=-1, keepdims=True))
    inv_std = lax.rsqrt(variance + EPS)
    return (centred * inv_std, inv_std)

def norm_back(grads, normal, inv_std):
    first = lax.optimization_barrier(jnp.mean(grads, axis=-1, keepdims=True))
    second = lax.optimization_barrier(jnp.mean(grads * normal, axis=-1, keepdims=True))
    return inv_std * (grads - first - normal * second)

def rounded(values):
    return lax.optimization_barrier(values.astype(jnp.bfloat16)).astype(jnp.float32)

def attend_image(projected, cot_image):
    factor = HEAD_DIM ** (-0.5)
    query_n, query_inv = row_norm(projected[:, 0])
    key_n, key_inv = row_norm(projected[:, 1])
    query_b = rounded(query_n)
    key_b = rounded(key_n)
    value_b = rounded(projected[:, 2])
    cot_f = cot_image.astype(jnp.float32)
    scores = jnp.einsum('phe,qhe->hpq', query_b, key_b) * factor
    expd = jnp.exp(scores)
    probs = expd / lax.optimization_barrier(jnp.sum(expd, axis=-1, keepdims=True))
    probs_b = rounded(probs)
    attended = jnp.einsum('hpq,qhe->phe', probs_b, value_b).astype(jnp.bfloat16)
    d_probs = jnp.einsum('phe,qhe->hpq', cot_f, value_b)
    d_value = jnp.einsum('hpq,phe->qhe', probs_b, cot_f)
    d_scores = rounded(probs * (d_probs - lax.optimization_barrier(jnp.sum(d_probs * probs, axis=-1, keepdims=True))))
    d_query = jnp.einsum('hpq,qhe->phe', d_scores, key_b) * factor
    d_key = jnp.einsum('hpq,phe->qhe', d_scores, query_b) * factor
    d_projected = jnp.stack([norm_back(d_query, query_n, query_inv), norm_back(d_key, key_n, key_inv), d_value], axis=1)
    return (attended, d_projected.astype(jnp.bfloat16))

def reference(tokens, w_qkv, cotangent):
    col_total = 3 * HEADS * HEAD_DIM
    centred, inv_std = row_norm(tokens.astype(jnp.float32))
    normed = centred.astype(jnp.bfloat16)
    flat_w = w_qkv.reshape(D, col_total)
    projected = jnp.dot(normed, flat_w, preferred_element_type=jnp.float32)
    images = TOKENS // PATCHES

    def per_image(paired):
        return attend_image(paired[0], paired[1])
    attended, d_projected = lax.map(per_image, (projected.reshape(images, PATCHES, 3, HEADS, HEAD_DIM), cotangent.reshape(images, PATCHES, HEADS, HEAD_DIM)))
    d_flat = d_projected.reshape(TOKENS, col_total)
    d_normed = lax.dot_general(d_flat, flat_w, (((1,), (1,)), ((), ())), preferred_element_type=jnp.float32)
    grad_tokens = norm_back(d_normed, centred, inv_std).astype(jnp.bfloat16)

    def add_block(block_idx, running):
        first_row = (block_idx * TOK_DEV).astype(jnp.int32)
        norm_block = lax.dynamic_slice_in_dim(normed, first_row, TOK_DEV, 0)
        grad_block = lax.dynamic_slice_in_dim(d_flat, first_row, TOK_DEV, 0)
        partial_w = lax.dot_general(norm_block, grad_block, (((0,), (0,)), ((), ())), preferred_element_type=jnp.float32)
        return running + rounded(partial_w)
    grad_w = lax.fori_loop(0, N_DP, add_block, jnp.zeros((D, col_total), jnp.float32))
    return (attended.reshape(TOKENS, HEADS * HEAD_DIM), grad_tokens, grad_w.astype(jnp.bfloat16).reshape(D, 3, HEADS * HEAD_DIM))
```

```python
import functools

import jax
import jax.numpy as jnp
from jax import lax
from jax.experimental import pallas as pl
from jax.experimental.pallas import tpu as pltpu
from jax.sharding import PartitionSpec as P

D = 6144
HEAD_DIM = 128
PATCHES = 256
TOK = 512
OWN = 384
COLS = 256
N_MP = 16
EPS = 1e-06
BF = jnp.bfloat16
F32 = jnp.float32
AXES = ("dp", "mp")
SPLIT = (2, 8, 2, 4, 2)


def coords(i):
    out = []
    for size in reversed(SPLIT):
        i, rest = divmod(i, size)
        out.append(rest)
    return list(reversed(out))


def index_of(c):
    i = 0
    for size, value in zip(SPLIT, c):
        i = i * size + value % size
    return i


NAMES = {"xl": 0, "z": 1, "xh": 2, "y": 3, "core": 4}


def send(value, turn=False, **shift):
    pairs = []
    for i in range(256):
        c = coords(i)
        sign = -1 if turn and c[4] else 1
        for name, by in shift.items():
            c[NAMES[name]] += sign * by
        pairs.append((i, index_of(c)))
    return lax.ppermute(value, AXES, pairs)


def after(value, *first):
    return lax.optimization_barrier((value, *first))[0]


N_MSG = 8


def gather_tokens(own):
    across = send(own, xh=1)
    ring = [own]
    for _ in range(3):
        ring.append(send(ring[-1], turn=True, y=1))
    ring.append(across)
    for _ in range(3):
        ring.append(send(ring[-1], turn=True, y=1))
    return ring + [send(m, core=1) for m in ring]


def dot(a, b, dims):
    return lax.dot_general(a, b, (dims, ((), ())), preferred_element_type=F32)


def head_norm(values):
    centred = values - jnp.mean(values, axis=-1, keepdims=True)
    inv = lax.rsqrt(jnp.mean(centred * centred, axis=-1, keepdims=True) + EPS)
    return centred * inv, inv


def head_norm_back(g, n, r):
    first = jnp.mean(g, axis=-1, keepdims=True)
    second = jnp.mean(g * n, axis=-1, keepdims=True)
    return r * (g - first - n * second)


def front_kernel(sc, *refs):
    msgs = refs[: 2 * N_MSG]
    w_hbm, cot, attended, d_proj, blocks, stats, gx = refs[2 * N_MSG : 2 * N_MSG + 7]
    xs, w, proj, w_sem, x_sem = refs[2 * N_MSG + 7 :]
    x_hi, y, core = sc[0], sc[1], sc[2]
    copies = []
    for m in range(2 * N_MSG):
        c = lax.rem(core + m // N_MSG, 2)
        row = lax.rem(y + (2 * c - 1) * (m % 4) + 4, 4)
        block = lax.rem(x_hi + m // 4 % 2, 2) * 8 + row * 2 + c
        at = pl.ds(pl.multiple_of(block * OWN, OWN), OWN)
        copies.append(pltpu.make_async_copy(msgs[m], xs.at[:, at], x_sem.at[m]))
    loads = [pltpu.make_async_copy(w_hbm.at[s], w.at[s], w_sem.at[s]) for s in range(3)]
    for copy in copies + loads:
        copy.start()
    for copy in copies:
        copy.wait()

    step = 16

    def norm_rows(i, carry):
        rows = pl.ds(pl.multiple_of(i * step, step), step)
        x = xs[rows, :].astype(F32)
        mean = jnp.sum(x, axis=-1, keepdims=True) * (1.0 / D)
        x = x - mean
        inv = lax.rsqrt(jnp.sum(x * x, axis=-1, keepdims=True) * (1.0 / D) + EPS)
        out = (x * inv).astype(BF)
        xs[rows, :] = out
        for j in range(N_MP):
            blocks[j, rows, :] = out[:, j * OWN : (j + 1) * OWN]
        lane = lax.broadcasted_iota(jnp.int32, (step, 128), 1)
        stats[rows, :] = jnp.where(lane == 0, mean, inv)
        return carry

    lax.fori_loop(0, TOK // step, norm_rows, 0)
    for s in range(3):
        loads[s].wait()
        proj[:, s * COLS : (s + 1) * COLS] = dot(xs[...], w[s], ((1,), (0,)))
    factor = HEAD_DIM ** (-0.5)
    for image in range(2):
        rows = slice(image * PATCHES, (image + 1) * PATCHES)
        total = jnp.zeros((PATCHES, HEAD_DIM), F32)
        for head in range(2):
            at = [slice(s * COLS + head * 128, s * COLS + head * 128 + 128) for s in range(3)]
            q, k, v = (proj[rows, c] for c in at)
            q_n, q_inv = head_norm(q)
            k_n, k_inv = head_norm(k)
            q_b, k_b, v_b = q_n.astype(BF), k_n.astype(BF), v.astype(BF)
            g = cot[rows, head * 128 : head * 128 + 128]
            e = jnp.exp(dot(q_b, k_b, ((1,), (1,))) * factor)
            p = e / jnp.sum(e, axis=-1, keepdims=True)
            p_b = p.astype(BF)
            attended[rows, head * 128 : head * 128 + 128] = dot(p_b, v_b, ((1,), (0,))).astype(BF)
            d_p = dot(g, v_b, ((1,), (1,)))
            d_v = dot(p_b, g, ((0,), (0,)))
            d_s = (p * (d_p - jnp.sum(d_p * p, axis=-1, keepdims=True))).astype(BF)
            d_q = dot(d_s, k_b, ((1,), (0,))) * factor
            d_k = dot(d_s, q_b, ((0,), (0,))) * factor
            parts = (head_norm_back(d_q, q_n, q_inv), head_norm_back(d_k, k_n, k_inv), d_v)
            for c, part, held in zip(at, parts, (q, k, v)):
                part = part.astype(BF)
                d_proj[rows, c] = part
                total = total + part.astype(F32) * held
        gx[rows, :] = total


VMEM = pl.BlockSpec(memory_space=pltpu.VMEM)
ANY = pl.BlockSpec(memory_space=pl.ANY)
SMEM = pl.BlockSpec(memory_space=pltpu.SMEM)


def params(mib=48):
    return pltpu.CompilerParams(vmem_limit_bytes=mib * 2**20)


def front(sc, msgs, w, cot):
    return pl.pallas_call(
        front_kernel,
        out_shape=(
            jax.ShapeDtypeStruct((TOK, COLS), BF),
            jax.ShapeDtypeStruct((TOK, 3 * COLS), BF),
            jax.ShapeDtypeStruct((N_MP, TOK, OWN), BF),
            jax.ShapeDtypeStruct((TOK, 128), F32),
            jax.ShapeDtypeStruct((TOK, 128), F32),
        ),
        in_specs=[SMEM] + [ANY] * (2 * N_MSG) + [ANY, VMEM],
        out_specs=(VMEM,) * 5,
        scratch_shapes=[
            pltpu.VMEM((TOK, D), BF),
            pltpu.VMEM((3, D, COLS), BF),
            pltpu.VMEM((TOK, 3 * COLS), F32),
            pltpu.SemaphoreType.DMA((3,)),
            pltpu.SemaphoreType.DMA((2 * N_MSG,)),
        ],
        compiler_params=params(),
        cost_estimate=pl.CostEstimate(
            flops=2 * TOK * D * 768, bytes_accessed=16 * 2**20, transcendentals=0
        ),
        name="front",
    )(sc, *msgs, w, cot)


def back_kernel(sc, d_proj, w, out, g):
    @pl.when(pl.program_id(0) == 0)
    def _():
        g[...] = jnp.zeros_like(g)

    d = sum(dot(d_proj[:, s * COLS : (s + 1) * COLS], w[s], ((1,), (1,))) for s in range(3))
    out[0] = d.astype(BF)
    g[...] += d[:, :128] + d[:, 128:256] + d[:, 256:]


def back(sc, d_proj, w, other):
    def block(i, s):
        x_hi = lax.rem(s[0] + i % 2, 2)
        return (0, x_hi * 8 + (i // 2) * 2 + lax.rem(s[2] + other, 2), 0)

    return pl.pallas_call(
        back_kernel,
        grid_spec=pltpu.PrefetchScalarGridSpec(
            num_scalar_prefetch=1,
            grid=(8,),
            in_specs=[
                pl.BlockSpec((TOK, 3 * COLS), lambda i, s: (0, 0)),
                pl.BlockSpec((3, OWN, COLS), block),
            ],
            out_specs=(
                pl.BlockSpec((1, TOK, OWN), lambda i, s: (i, 0, 0)),
                pl.BlockSpec((TOK, 128), lambda i, s: (0, 0)),
            ),
        ),
        out_shape=(
            jax.ShapeDtypeStruct((8, TOK, OWN), BF),
            jax.ShapeDtypeStruct((TOK, 128), F32),
        ),
        compiler_params=params(24),
        cost_estimate=pl.CostEstimate(
            flops=TOK * D * 768, bytes_accessed=8 * 2**20, transcendentals=0
        ),
        name="back",
    )(sc, d_proj, w)


def target(s, step):
    return lax.rem(s[4] + (2 * s[2] - 1) * (1 + step) + 16, 8)


def qk_kernel(with_sum, sc, n, d_qk, *refs):
    out = refs[-1]
    for part in range(2):
        rows = dot(n[0], d_qk[:, part * COLS : (part + 1) * COLS], ((0,), (0,)))
        if with_sum:
            rows = rows + refs[0][0, part].astype(F32)
        out[0, part] = rows.astype(BF)


def qk_step(sc, blocks, d_proj, sums, step, slots=(0, 2)):
    first, count = slots[0], slots[1] - slots[0]

    def chunk(first):
        return pl.BlockSpec((1, 2, OWN, COLS), lambda i, s: (i + first, 0, 0, 0))

    return pl.pallas_call(
        functools.partial(qk_kernel, bool(sums)),
        grid_spec=pltpu.PrefetchScalarGridSpec(
            num_scalar_prefetch=1,
            grid=(count,),
            in_specs=[
                pl.BlockSpec(
                    (1, TOK, OWN),
                    lambda i, s: (lax.rem(s[3] + 1 + i + first, 2) * 8 + target(s, step), 0, 0),
                ),
                pl.BlockSpec((TOK, 2 * COLS), lambda i, s: (0, 0)),
            ]
            + [chunk(first) for _ in sums],
            out_specs=chunk(0),
        ),
        out_shape=jax.ShapeDtypeStruct((count, 2, OWN, COLS), BF),
        compiler_params=params(16),
        cost_estimate=pl.CostEstimate(
            flops=4 * count * TOK * OWN * COLS, bytes_accessed=4 * 2**20, transcendentals=0
        ),
        name="query_key_rows",
    )(sc, blocks, d_proj, *sums)


def v_kernel(with_sum, sc, n, d_v, *refs):
    rows = dot(n[0], d_v[...], ((0,), (0,)))
    for ref in refs[:-1]:
        rows = rows + ref[0].astype(F32)
    refs[-1][0] = rows.astype(BF)


def v_rows(sc, blocks, d_proj, sums, steps, far):
    first = steps[0]
    chunk = lambda at: pl.BlockSpec((1, OWN, COLS), lambda i, s: (i + at, 0, 0))
    return pl.pallas_call(
        functools.partial(v_kernel, bool(sums)),
        grid_spec=pltpu.PrefetchScalarGridSpec(
            num_scalar_prefetch=1,
            grid=(len(steps),),
            in_specs=[
                pl.BlockSpec(
                    (1, TOK, OWN),
                    lambda i, s: (lax.rem(s[3] + far, 2) * 8 + target(s, first + i), 0, 0),
                ),
                pl.BlockSpec((TOK, COLS), lambda i, s: (0, 2)),
            ]
            + [chunk(at) for _, at in sums],
            out_specs=chunk(0),
        ),
        out_shape=jax.ShapeDtypeStruct((len(steps), OWN, COLS), BF),
        compiler_params=params(16),
        cost_estimate=pl.CostEstimate(
            flops=2 * len(steps) * TOK * OWN * COLS, bytes_accessed=2 * 2**20, transcendentals=0
        ),
        name="value_rows",
    )(sc, blocks, d_proj, *[a for a, _ in sums])


Y_GROUPS = [[x * 8 + y * 2 + c for y in range(4)] for x in range(2) for c in range(2)]


def local(tokens, w_qkv, cotangent):
    dp = lax.axis_index("dp")
    mp = lax.axis_index("mp")
    sc = jnp.stack([mp // 8, mp % 8 // 2, mp % 2, dp // 8, dp % 8, mp]).astype(jnp.int32)
    w = jnp.transpose(w_qkv, (1, 0, 2))
    msgs = gather_tokens(tokens)
    attended, d_proj, blocks, stats, gx = front(sc, msgs, w, cotangent)

    qk = qk_step(sc, blocks, d_proj, (), 0)
    d_far = after(d_proj, qk)
    qk = send(qk, turn=True, z=1)
    far = [v_rows(sc, blocks, d_far, (), range(4 * i, 4 * i + 4), 1) for i in range(2)]
    d_back = after(d_far, *far)
    far = [send(f, xl=1) for f in far]

    theirs, g_theirs = back(sc, d_back, w, 1)
    d_back = after(d_back, theirs)
    theirs = send(theirs, core=1)
    mine, g_mine = back(sc, d_back, w, 0)
    sums = jnp.stack([jnp.sum(g_theirs + g_mine, axis=-1), jnp.sum(gx, axis=-1)]).reshape(8, 128)
    for shift in ({"core": 1}, {"xh": 1}, {"y": 1}, {"y": 2}):
        sums = sums + send(sums, **shift)
    pair = (theirs.astype(F32) + mine.astype(F32)).astype(BF).reshape(8 * TOK, OWN)
    over_y = lax.psum_scatter(
        pair, "mp", scatter_dimension=0, tiled=True, axis_index_groups=Y_GROUPS
    )

    def v_ring(step, v, qk):
        sums = [(far[step // 4], step % 4)] + ([] if v is None else [(v, 0)])
        return v_rows(sc, blocks, after(d_proj, qk), sums, (step,), 0)

    v = None
    for step in range(1, 7):
        qk = qk_step(sc, blocks, d_proj, (qk,), step)
        if step >= 2:
            held = v_ring(step - 2, v, qk)
            v = send(held, turn=True, z=1)
            qk = after(qk, held)
        qk = send(qk, turn=True, z=1)
    away = qk_step(sc, blocks, d_proj, (qk,), 7, (0, 1))
    away = send(away, xl=1)
    home = qk_step(sc, blocks, d_proj, (qk,), 7, (1, 2))
    for step in range(5, 8):
        v = v_ring(step, v, home)
        if step < 7:
            v = send(v, turn=True, z=1)
    qk = (home[0].astype(F32) + away[0].astype(F32)).astype(BF)
    grad_w = jnp.transpose(jnp.concatenate([qk, v]), (1, 0, 2))

    d_own = over_y[:TOK].astype(F32) + send(over_y[TOK:], xh=1).astype(F32)
    sums = sums.reshape(2, TOK, 1) * (1.0 / D)
    mean, inv = stats[:, 0:1], stats[:, 1:2]
    centred = (tokens.astype(F32) - mean) * inv
    grad_tokens = (inv * (d_own - sums[0] - centred * sums[1])).astype(BF)
    return attended, grad_tokens, grad_w


def solution(mesh):
    return jax.shard_map(
        local,
        mesh=mesh,
        in_specs=(P("dp", "mp"), P(None, None, "mp"), P("dp", "mp")),
        out_specs=(P("dp", "mp"), P("dp", "mp"), P("dp", None, "mp")),
        check_vma=False,
    )
```

```python
import functools

import jax
import jax.numpy as jnp
from jax import lax
from jax.experimental import pallas as pl
from jax.experimental.pallas import tpu as pltpu
from jax.sharding import PartitionSpec as P

D = 6144
HEAD_DIM = 128
PATCHES = 256
TOK = 512
OWN = 384
COLS = 256
N_MP = 16
EPS = 1e-06
SCALE = 0.1
BF = jnp.bfloat16
F32 = jnp.float32
AXES = ("dp", "mp")
SPLIT = (2, 8, 2, 4, 2)


def coords(i):
    out = []
    for size in reversed(SPLIT):
        i, rest = divmod(i, size)
        out.append(rest)
    return list(reversed(out))


def index_of(c):
    i = 0
    for size, value in zip(SPLIT, c):
        i = i * size + value % size
    return i


NAMES = {"xl": 0, "z": 1, "xh": 2, "y": 3, "core": 4}


def send(value, turn=False, **shift):
    pairs = []
    for i in range(256):
        c = coords(i)
        sign = -1 if turn and c[4] else 1
        for name, by in shift.items():
            c[NAMES[name]] += sign * by
        pairs.append((i, index_of(c)))
    return lax.ppermute(value, AXES, pairs)


def after(value, *first):
    return lax.optimization_barrier((value, *first))[0]


PIECES = (
    (0, 0, 0, 512, 0, 0),
    (1, 0, 0, 512, 0, 3),
    (2, 0, 0, 512, 0, 1),
    (3, 0, 0, 512, 0, 2),
    (4, 0, 0, 512, 1, 0),
    (5, 0, 256, 256, 1, 3),
    (5, 256, 256, 256, 1, 1),
    (6, 0, 0, 256, 1, 3),
    (7, 0, 0, 256, 1, 1),
    (8, 0, 256, 256, 1, 2),
    (9, 0, 0, 256, 1, 2),
)
N_MSG = 10
N_COPY = 2 * len(PIECES)


def gather_tokens(own):
    x = send(own, xh=1)
    a = send(own, y=1)
    b = send(own, y=-1)
    d = send(own, y=2)
    ab = send(jnp.concatenate([a[256:], b[256:]]), xh=1)
    low = x[:256]
    xa = send(low, y=1)
    xb = send(low, y=-1)
    xd = send(low, y=2)
    dx = send(d[256:], xh=1)
    mine = [own, a, b, d, x, ab, xa, xb, dx, xd]
    return mine + [send(m, core=1) for m in mine]


def dot(a, b, dims):
    return lax.dot_general(a, b, (dims, ((), ())), preferred_element_type=F32)


def head_norm(values):
    centred = values - jnp.mean(values, axis=-1, keepdims=True)
    inv = lax.rsqrt(jnp.mean(centred * centred, axis=-1, keepdims=True) + EPS)
    return centred * inv, inv


def head_norm_back(g, n, r):
    first = jnp.mean(g, axis=-1, keepdims=True)
    second = jnp.mean(g * n, axis=-1, keepdims=True)
    return r * (g - first - n * second)


def front_kernel(sc, *refs):
    msgs = refs[: 2 * N_MSG]
    w_hbm, cot, attended, d_proj, blocks, stats, gx = refs[2 * N_MSG : 2 * N_MSG + 7]
    xs, w, proj, w_sem, x_sem, b_sem = refs[2 * N_MSG + 7 :]
    x_hi, y, core = sc[0], sc[1], sc[2]
    copies = []
    for i in range(N_COPY):
        other, (m, src, row, rows, dx, dy) = i // len(PIECES), PIECES[i % len(PIECES)]
        block = lax.rem(x_hi + dx, 2) * 8 + lax.rem(y + dy, 4) * 2 + lax.rem(core + other, 2)
        at = pl.ds(pl.multiple_of(block * OWN, OWN), OWN)
        copies.append(
            pltpu.make_async_copy(
                msgs[other * N_MSG + m].at[pl.ds(src, rows)],
                xs.at[pl.ds(row, rows), at],
                x_sem.at[i],
            )
        )
    loads = [pltpu.make_async_copy(w_hbm.at[s], w.at[s], w_sem.at[s]) for s in range(3)]
    for copy in copies + loads:
        copy.start()
    for copy in copies:
        copy.wait()

    step = 16

    def norm_rows(i, carry):
        rows = pl.ds(pl.multiple_of(i * step, step), step)
        x = xs[rows, :].astype(F32)
        mean = jnp.sum(x, axis=-1, keepdims=True) * (1.0 / D)
        x = x - mean
        inv = lax.rsqrt(jnp.sum(x * x, axis=-1, keepdims=True) * (1.0 / D) + EPS)
        out = (x * inv).astype(BF)
        xs[rows, :] = out
        lane = lax.broadcasted_iota(jnp.int32, (step, 128), 1)
        stats[rows, :] = jnp.where(lane == 0, mean, inv)
        return carry

    lax.fori_loop(0, TOK // step, norm_rows, 0)
    leaving = [
        pltpu.make_async_copy(xs.at[:, j * OWN : (j + 1) * OWN], blocks.at[j], b_sem.at[j])
        for j in range(N_MP)
    ]
    for copy in leaving:
        copy.start()
    for s in range(3):
        loads[s].wait()
        proj[:, s * COLS : (s + 1) * COLS] = dot(xs[...], w[s], ((1,), (0,)))
    factor = HEAD_DIM ** (-0.5)
    for image in range(2):
        rows = slice(image * PATCHES, (image + 1) * PATCHES)
        total = jnp.zeros((PATCHES, HEAD_DIM), F32)
        for head in range(2):
            at = [slice(s * COLS + head * 128, s * COLS + head * 128 + 128) for s in range(3)]
            q, k, v = (proj[rows, c] for c in at)
            q_n, q_inv = head_norm(q)
            k_n, k_inv = head_norm(k)
            q_b, k_b, v_b = q_n.astype(BF), k_n.astype(BF), v.astype(BF)
            g = cot[rows, head * 128 : head * 128 + 128]
            e = jnp.exp(dot(q_b, k_b, ((1,), (1,))) * factor)
            p = e / jnp.sum(e, axis=-1, keepdims=True)
            p_b = p.astype(BF)
            attended[rows, head * 128 : head * 128 + 128] = dot(p_b, v_b, ((1,), (0,))).astype(BF)
            d_p = dot(g, v_b, ((1,), (1,)))
            d_v = dot(p_b, g, ((0,), (0,)))
            d_s = (p * (d_p - jnp.sum(d_p * p, axis=-1, keepdims=True))).astype(BF)
            d_q = dot(d_s, k_b, ((1,), (0,))) * factor
            d_k = dot(d_s, q_b, ((0,), (0,))) * factor
            parts = (head_norm_back(d_q, q_n, q_inv), head_norm_back(d_k, k_n, k_inv), d_v)
            for c, part, held in zip(at, parts, (q, k, v)):
                part = part.astype(BF)
                d_proj[rows, c] = part
                total = total + part.astype(F32) * held
        gx[rows, :] = total
    for copy in leaving:
        copy.wait()


VMEM = pl.BlockSpec(memory_space=pltpu.VMEM)
ANY = pl.BlockSpec(memory_space=pl.ANY)
HBM = pl.BlockSpec(memory_space=pltpu.HBM)
SMEM = pl.BlockSpec(memory_space=pltpu.SMEM)


def cost(us):
    return pl.CostEstimate(flops=int(us * 1e9 * SCALE), bytes_accessed=1000, transcendentals=0)


def params(mib=48):
    return pltpu.CompilerParams(vmem_limit_bytes=mib * 2**20)


def front(sc, msgs, w, cot):
    return pl.pallas_call(
        front_kernel,
        out_shape=(
            jax.ShapeDtypeStruct((TOK, COLS), BF),
            jax.ShapeDtypeStruct((TOK, 3 * COLS), BF),
            jax.ShapeDtypeStruct((N_MP, TOK, OWN), BF),
            jax.ShapeDtypeStruct((TOK, 128), F32),
            jax.ShapeDtypeStruct((TOK, 128), F32),
        ),
        in_specs=[SMEM] + [ANY] * (2 * N_MSG) + [HBM, VMEM],
        out_specs=(VMEM, VMEM, HBM, VMEM, VMEM),
        scratch_shapes=[
            pltpu.VMEM((TOK, D), BF),
            pltpu.VMEM((3, D, COLS), BF),
            pltpu.VMEM((TOK, 3 * COLS), F32),
            pltpu.SemaphoreType.DMA((3,)),
            pltpu.SemaphoreType.DMA((N_COPY,)),
            pltpu.SemaphoreType.DMA((N_MP,)),
        ],
        compiler_params=params(),
        cost_estimate=cost(25),
        name="front",
    )(sc, *msgs, w, cot)


def back_kernel(sc, d_proj, w, out, g):
    @pl.when(pl.program_id(0) == 0)
    def _():
        g[...] = jnp.zeros_like(g)

    d = sum(dot(d_proj[:, s * COLS : (s + 1) * COLS], w[s], ((1,), (1,))) for s in range(3))
    out[0] = d.astype(BF)
    g[...] += d[:, :128] + d[:, 128:256] + d[:, 256:]


def back(sc, d_proj, w, other):
    def block(i, s):
        x_hi = lax.rem(s[0] + i % 2, 2)
        y = lax.rem(s[1] + i // 2, 4)
        return (0, x_hi * 8 + y * 2 + lax.rem(s[2] + other, 2), 0)

    return pl.pallas_call(
        back_kernel,
        grid_spec=pltpu.PrefetchScalarGridSpec(
            num_scalar_prefetch=1,
            grid=(8,),
            in_specs=[
                pl.BlockSpec((TOK, 3 * COLS), lambda i, s: (0, 0)),
                pl.BlockSpec((3, OWN, COLS), block),
            ],
            out_specs=(
                pl.BlockSpec((1, TOK, OWN), lambda i, s: (i, 0, 0)),
                pl.BlockSpec((TOK, 128), lambda i, s: (0, 0)),
            ),
        ),
        out_shape=(
            jax.ShapeDtypeStruct((8, TOK, OWN), BF),
            jax.ShapeDtypeStruct((TOK, 128), F32),
        ),
        compiler_params=params(57),
        cost_estimate=cost(6),
        name="back",
    )(sc, d_proj, w)


HOPS = (4, -3, 3, -2, 2, -1, 1, 0)


def target(s, hop):
    return lax.rem(s[4] + (1 - 2 * s[2]) * hop + 8, 8)


def rows_kernel(hops, sides, parts, firsts, sc, blocks, d_proj, *refs):
    slots, n_sums = len(hops), len(firsts)
    sums = refs[:n_sums]
    out, n, d, held, n_sem, d_sem, s_sem = refs[n_sums:]
    copies = []
    for i, (hop, side) in enumerate(zip(hops, sides)):
        block = lax.rem(sc[3] + side, 2) * 8 + target(sc, hop)
        copies.append(pltpu.make_async_copy(blocks.at[block], n.at[i], n_sem.at[i]))
    width = len(parts) * COLS
    copies.append(pltpu.make_async_copy(d_proj.at[:, pl.ds(parts[0] * COLS, width)], d, d_sem))
    for j in range(n_sums):
        copies.append(
            pltpu.make_async_copy(sums[j].at[pl.ds(firsts[j], slots)], held.at[j], s_sem.at[j])
        )
    for copy in copies:
        copy.start()
    for copy in copies[slots:]:
        copy.wait()
    for i in range(slots):
        copies[i].wait()
        rows = dot(n[i], d[...], ((0,), (0,)))
        for j in range(n_sums):
            rows = rows + held[j, i].astype(F32)
        out[i] = rows.astype(BF)


def rows_step(sc, blocks, d_proj, sums, hops, sides, parts):
    slots, n_sums, width = len(hops), len(sums), len(parts) * COLS
    return pl.pallas_call(
        functools.partial(rows_kernel, hops, sides, parts, tuple(at for _, at in sums)),
        in_specs=[SMEM, HBM, ANY] + [ANY] * n_sums,
        out_specs=VMEM,
        out_shape=jax.ShapeDtypeStruct((slots, OWN, width), BF),
        scratch_shapes=[
            pltpu.VMEM((slots, TOK, OWN), BF),
            pltpu.VMEM((TOK, width), BF),
            pltpu.VMEM((max(n_sums, 1), slots, OWN, width), BF),
            pltpu.SemaphoreType.DMA((slots,)),
            pltpu.SemaphoreType.DMA(()),
            pltpu.SemaphoreType.DMA((max(n_sums, 1),)),
        ],
        compiler_params=params(57),
        cost_estimate=cost(1 + 0.4 * slots * len(parts)),
        name="weight_rows",
    )(sc, blocks, d_proj, *[a for a, _ in sums])


def local(tokens, w_qkv, cotangent):
    dp = lax.axis_index("dp")
    mp = lax.axis_index("mp")
    sc = jnp.stack([mp // 8, mp % 8 // 2, mp % 2, dp // 8, dp % 8, mp]).astype(jnp.int32)
    w = jnp.transpose(w_qkv, (1, 0, 2))
    msgs = gather_tokens(tokens)
    attended, d_proj, blocks, stats, gx = front(sc, msgs, w, cotangent)

    turn = gx

    def rows(sums, hops, sides, parts):
        nonlocal turn
        turn = rows_step(sc, blocks, after(d_proj, turn), sums, hops, sides, parts)
        return turn

    def pass_on(sums, hop, value):
        if value:
            own = (far[HOPS.index(hop) // 4], HOPS.index(hop) % 4)
            out = rows((own, *sums), (hop,), (0,), (2,))
        else:
            out = rows(sums, (hop, hop), (1, 0), (0, 1))
        return send(out, turn=True, z=1 if hop > 0 else -1)

    long = pass_on((), 4, False)
    short = pass_on((), -3, False)
    far = [send(rows((), HOPS[i : i + 4], (1,) * 4, (2,)), xl=1) for i in (0, 4)]
    long = pass_on(((long, 0),), 3, False)

    theirs, g_theirs = back(sc, after(d_proj, turn), w, 1)
    turn = theirs
    theirs = send(theirs, core=1)
    short = pass_on(((short, 0),), -2, False)
    mine, g_mine = back(sc, after(d_proj, turn), w, 0)
    pairs = [
        (theirs[2 * i : 2 * i + 2].astype(F32) + mine[2 * i : 2 * i + 2].astype(F32)).astype(BF)
        for i in range(4)
    ]
    turn = pairs[1]
    over_y = [pairs[0]] + [send(pairs[i], y=i) for i in range(1, 4)]
    v_long = pass_on((), 4, True)
    v_short = pass_on((), -3, True)
    sums = jnp.stack([jnp.sum(g_theirs + g_mine, axis=-1), jnp.sum(gx, axis=-1)]).reshape(8, 128)

    long = pass_on(((long, 0),), 2, False)
    short = pass_on(((short, 0),), -1, False)
    v_long = pass_on(((v_long, 0),), 3, True)
    v_short = pass_on(((v_short, 0),), -2, True)
    for shift in ({"core": 1}, {"xh": 1}, {"y": 1}, {"y": 2}):
        sums = sums + send(sums, **shift)
    turn = after(turn, sums)
    long = pass_on(((long, 0),), 1, False)
    v_long = pass_on(((v_long, 0),), 2, True)
    v_short = pass_on(((v_short, 0),), -1, True)
    over_y = sum(o.astype(F32) for o in over_y)
    across = over_y[1].astype(BF)
    turn = after(turn, across)
    across = send(across, xh=1)
    v_long = pass_on(((v_long, 0),), 1, True)
    v_short = ((v_short, 0),)
    away = send(rows(((long, 0), (short, 0)), (0,), (1,), (0, 1)), xl=1)
    home = rows(((long, 1), (short, 1)), (0,), (0,), (0, 1))
    v = rows(((far[1], 3), (v_long, 0), *v_short), (0,), (0,), (2,))
    qk = (home[0].astype(F32) + away[0].astype(F32)).astype(BF)
    grad_w = jnp.stack([qk[:, :COLS], qk[:, COLS:], v[0]])
    grad_w = jnp.transpose(grad_w, (1, 0, 2))

    d_own = over_y[0] + across.astype(F32)
    sums = sums.reshape(2, TOK, 1) * (1.0 / D)
    mean, inv = stats[:, 0:1], stats[:, 1:2]
    centred = (tokens.astype(F32) - mean) * inv
    grad_tokens = (inv * (d_own - sums[0] - centred * sums[1])).astype(BF)
    return attended, grad_tokens, grad_w


def solution(mesh):
    return jax.shard_map(
        local,
        mesh=mesh,
        in_specs=(P("dp", "mp"), P(None, None, "mp"), P("dp", "mp")),
        out_specs=(P("dp", "mp"), P("dp", "mp"), P("dp", None, "mp")),
        check_vma=False,
    )
```

```python
import functools

import jax
import jax.numpy as jnp
from jax import lax
from jax.experimental import pallas as pl
from jax.experimental.pallas import tpu as pltpu
from jax.sharding import PartitionSpec as P

D = 6144
HEAD_DIM = 128
PATCHES = 256
TOK = 512
OWN = 384
COLS = 256
N_MP = 16
EPS = 1e-06
SCALE = 0.1
BF = jnp.bfloat16
F32 = jnp.float32
AXES = ("dp", "mp")
SPLIT = (2, 8, 2, 4, 2)


def coords(i):
    out = []
    for size in reversed(SPLIT):
        i, rest = divmod(i, size)
        out.append(rest)
    return list(reversed(out))


def index_of(c):
    i = 0
    for size, value in zip(SPLIT, c):
        i = i * size + value % size
    return i


NAMES = {"xl": 0, "z": 1, "xh": 2, "y": 3, "core": 4}


def send(value, turn=False, **shift):
    pairs = []
    for i in range(256):
        c = coords(i)
        sign = -1 if turn and c[4] else 1
        for name, by in shift.items():
            c[NAMES[name]] += sign * by
        pairs.append((i, index_of(c)))
    return lax.ppermute(value, AXES, pairs)


def after(value, *first):
    return lax.optimization_barrier((value, *first))[0]


PIECES = (
    (0, 0, 0, 512, 0, 0),
    (1, 0, 0, 512, 0, 3),
    (2, 0, 0, 512, 0, 1),
    (3, 0, 0, 512, 0, 2),
    (4, 0, 0, 512, 1, 0),
    (5, 0, 256, 256, 1, 3),
    (5, 256, 256, 256, 1, 1),
    (6, 0, 0, 256, 1, 3),
    (7, 0, 0, 256, 1, 1),
    (8, 0, 256, 256, 1, 2),
    (9, 0, 0, 256, 1, 2),
)
N_MSG = 10
N_COPY = 2 * len(PIECES)


def gather_tokens(own):
    x = send(own, xh=1)
    a = send(own, y=1)
    b = send(own, y=-1)
    d = send(after(own, x), y=2)
    ab = send(jnp.concatenate([a[256:], b[256:]]), xh=1)
    low = x[:256]
    xa = send(low, y=1)
    xb = send(low, y=-1)
    xd = send(low, y=2)
    dx = send(d[256:], xh=1)
    mine = [own, a, b, d, x, ab, xa, xb, dx, xd]
    return mine + [send(m, core=1) for m in mine]


def dot(a, b, dims):
    return lax.dot_general(a, b, (dims, ((), ())), preferred_element_type=F32)


def head_norm(values):
    centred = values - jnp.mean(values, axis=-1, keepdims=True)
    inv = lax.rsqrt(jnp.mean(centred * centred, axis=-1, keepdims=True) + EPS)
    return centred * inv, inv


def head_norm_back(g, n, r):
    first = jnp.mean(g, axis=-1, keepdims=True)
    second = jnp.mean(g * n, axis=-1, keepdims=True)
    return r * (g - first - n * second)


def front_kernel(sc, *refs):
    msgs = refs[: 2 * N_MSG]
    w_hbm, cot, attended, d_proj, blocks, stats, gx = refs[2 * N_MSG : 2 * N_MSG + 7]
    xs, w, proj, w_sem, x_sem, b_sem = refs[2 * N_MSG + 7 :]
    x_hi, y, core = sc[0], sc[1], sc[2]
    copies = []
    for i in range(N_COPY):
        other, (m, src, row, rows, dx, dy) = i // len(PIECES), PIECES[i % len(PIECES)]
        block = lax.rem(x_hi + dx, 2) * 8 + lax.rem(y + dy, 4) * 2 + lax.rem(core + other, 2)
        at = pl.ds(pl.multiple_of(block * OWN, OWN), OWN)
        copies.append(
            pltpu.make_async_copy(
                msgs[other * N_MSG + m].at[pl.ds(src, rows)],
                xs.at[pl.ds(row, rows), at],
                x_sem.at[i],
            )
        )
    loads = [pltpu.make_async_copy(w_hbm.at[s], w.at[s], w_sem.at[s]) for s in range(3)]
    for copy in copies + loads:
        copy.start()
    for copy in copies:
        copy.wait()

    step = 16

    def norm_rows(i, carry):
        rows = pl.ds(pl.multiple_of(i * step, step), step)
        x = xs[rows, :].astype(F32)
        mean = jnp.sum(x, axis=-1, keepdims=True) * (1.0 / D)
        x = x - mean
        inv = lax.rsqrt(jnp.sum(x * x, axis=-1, keepdims=True) * (1.0 / D) + EPS)
        out = (x * inv).astype(BF)
        xs[rows, :] = out
        lane = lax.broadcasted_iota(jnp.int32, (step, 128), 1)
        stats[rows, :] = jnp.where(lane == 0, mean, inv)
        return carry

    lax.fori_loop(0, TOK // step, norm_rows, 0)
    leaving = [
        pltpu.make_async_copy(xs.at[:, j * OWN : (j + 1) * OWN], blocks.at[j], b_sem.at[j])
        for j in range(N_MP)
    ]
    for copy in leaving:
        copy.start()
    for s in range(3):
        loads[s].wait()
        proj[:, s * COLS : (s + 1) * COLS] = dot(xs[...], w[s], ((1,), (0,)))
    factor = HEAD_DIM ** (-0.5)
    for image in range(2):
        rows = slice(image * PATCHES, (image + 1) * PATCHES)
        total = jnp.zeros((PATCHES, HEAD_DIM), F32)
        for head in range(2):
            at = [slice(s * COLS + head * 128, s * COLS + head * 128 + 128) for s in range(3)]
            q, k, v = (proj[rows, c] for c in at)
            q_n, q_inv = head_norm(q)
            k_n, k_inv = head_norm(k)
            q_b, k_b, v_b = q_n.astype(BF), k_n.astype(BF), v.astype(BF)
            g = cot[rows, head * 128 : head * 128 + 128]
            e = jnp.exp(dot(q_b, k_b, ((1,), (1,))) * factor)
            p = e / jnp.sum(e, axis=-1, keepdims=True)
            p_b = p.astype(BF)
            attended[rows, head * 128 : head * 128 + 128] = dot(p_b, v_b, ((1,), (0,))).astype(BF)
            d_p = dot(g, v_b, ((1,), (1,)))
            d_v = dot(p_b, g, ((0,), (0,)))
            d_s = (p * (d_p - jnp.sum(d_p * p, axis=-1, keepdims=True))).astype(BF)
            d_q = dot(d_s, k_b, ((1,), (0,))) * factor
            d_k = dot(d_s, q_b, ((0,), (0,))) * factor
            parts = (head_norm_back(d_q, q_n, q_inv), head_norm_back(d_k, k_n, k_inv), d_v)
            for c, part, held in zip(at, parts, (q, k, v)):
                part = part.astype(BF)
                d_proj[rows, c] = part
                total = total + part.astype(F32) * held
        gx[rows, :] = total
    for copy in leaving:
        copy.wait()


VMEM = pl.BlockSpec(memory_space=pltpu.VMEM)
ANY = pl.BlockSpec(memory_space=pl.ANY)
HBM = pl.BlockSpec(memory_space=pltpu.HBM)
SMEM = pl.BlockSpec(memory_space=pltpu.SMEM)


def cost(us):
    return pl.CostEstimate(flops=int(us * 1e9 * SCALE), bytes_accessed=1000, transcendentals=0)


def params(mib=60):
    return pltpu.CompilerParams(vmem_limit_bytes=mib * 2**20)


def front(sc, msgs, w, cot):
    return pl.pallas_call(
        front_kernel,
        out_shape=(
            jax.ShapeDtypeStruct((TOK, COLS), BF),
            jax.ShapeDtypeStruct((TOK, 3 * COLS), BF),
            jax.ShapeDtypeStruct((N_MP, TOK, OWN), BF),
            jax.ShapeDtypeStruct((TOK, 128), F32),
            jax.ShapeDtypeStruct((TOK, 128), F32),
        ),
        in_specs=[SMEM] + [HBM] * (2 * N_MSG) + [HBM, VMEM],
        out_specs=(VMEM, VMEM, HBM, VMEM, VMEM),
        scratch_shapes=[
            pltpu.VMEM((TOK, D), BF),
            pltpu.VMEM((3, D, COLS), BF),
            pltpu.VMEM((TOK, 3 * COLS), F32),
            pltpu.SemaphoreType.DMA((3,)),
            pltpu.SemaphoreType.DMA((N_COPY,)),
            pltpu.SemaphoreType.DMA((N_MP,)),
        ],
        compiler_params=params(),
        cost_estimate=cost(25),
        name="front",
    )(sc, *msgs, w, cot)


def back_kernel(sc, d_proj, w, out, g):
    @pl.when(pl.program_id(0) == 0)
    def _():
        g[...] = jnp.zeros_like(g)

    d = sum(dot(d_proj[:, s * COLS : (s + 1) * COLS], w[s], ((1,), (1,))) for s in range(3))
    out[0] = d.astype(BF)
    g[...] += d[:, :128] + d[:, 128:256] + d[:, 256:]


def back(sc, d_proj, w, other):
    def block(i, s):
        x_hi = lax.rem(s[0] + i % 2, 2)
        y = lax.rem(s[1] + i // 2, 4)
        return (0, x_hi * 8 + y * 2 + lax.rem(s[2] + other, 2), 0)

    return pl.pallas_call(
        back_kernel,
        grid_spec=pltpu.PrefetchScalarGridSpec(
            num_scalar_prefetch=1,
            grid=(8,),
            in_specs=[
                pl.BlockSpec((TOK, 3 * COLS), lambda i, s: (0, 0)),
                pl.BlockSpec((3, OWN, COLS), block),
            ],
            out_specs=(
                pl.BlockSpec((1, TOK, OWN), lambda i, s: (i, 0, 0)),
                pl.BlockSpec((TOK, 128), lambda i, s: (0, 0)),
            ),
        ),
        out_shape=(
            jax.ShapeDtypeStruct((8, TOK, OWN), BF),
            jax.ShapeDtypeStruct((TOK, 128), F32),
        ),
        compiler_params=params(24),
        cost_estimate=cost(6),
        name="back",
    )(sc, d_proj, w)


def rows_kernel(with_far, sc, n, d, *refs):
    rows = dot(n[0], d[...], ((0,), (0,)))
    if with_far:
        rows = rows + refs[0][0].astype(F32)
    refs[-1][0] = rows.astype(BF)


def weight_rows(sc, blocks, d_proj, width, at, sides, far=None):
    chunk = lambda: pl.BlockSpec((1, OWN, width), lambda i, s: (i, 0, 0))
    n_sides = len(sides)

    def block(i, s):
        side = lax.rem(i, 2) if n_sides == 2 else sides[0]
        return (lax.rem(s[3] + side, 2) * 8 + i // n_sides, 0, 0)

    return pl.pallas_call(
        functools.partial(rows_kernel, far is not None),
        grid_spec=pltpu.PrefetchScalarGridSpec(
            num_scalar_prefetch=1,
            grid=(8 * n_sides,),
            in_specs=[
                pl.BlockSpec((1, TOK, OWN), block),
                pl.BlockSpec((TOK, width), lambda i, s: (0, at)),
            ]
            + ([] if far is None else [chunk()]),
            out_specs=chunk(),
        ),
        out_shape=jax.ShapeDtypeStruct((8 * n_sides, OWN, width), BF),
        compiler_params=params(20),
        cost_estimate=cost(2.0 * n_sides),
        name="weight_rows",
    )(sc, blocks, d_proj, *([] if far is None else [far]))


def gather_kernel(near, other, far, out):
    for part in range(2):
        at = slice(part * COLS, (part + 1) * COLS)
        out[part] = (near[:, at].astype(F32) + other[:, at].astype(F32)).astype(BF)
    out[2] = far[...]


def grad_rows(near, other, far):
    whole = lambda *shape: pl.BlockSpec(shape, lambda i: (0,) * len(shape))
    return pl.pallas_call(
        gather_kernel,
        grid=(1,),
        in_specs=[whole(OWN, 2 * COLS), whole(OWN, 2 * COLS), whole(OWN, COLS)],
        out_specs=whole(3, OWN, COLS),
        out_shape=jax.ShapeDtypeStruct((3, OWN, COLS), BF),
        compiler_params=params(16),
        cost_estimate=cost(1),
        name="grad_rows",
    )(near, other, far)


Z_GROUPS = [list(range(8)), list(range(8, 16))]


def sum_over_z(rows):
    rows = rows.reshape(-1, rows.shape[-1])
    return lax.psum_scatter(
        rows, "dp", scatter_dimension=0, tiled=True, axis_index_groups=Z_GROUPS
    )


def local(tokens, w_qkv, cotangent):
    dp = lax.axis_index("dp")
    mp = lax.axis_index("mp")
    sc = jnp.stack([mp // 8, mp % 8 // 2, mp % 2, dp // 8, dp % 8, mp]).astype(jnp.int32)
    w = jnp.transpose(w_qkv, (1, 0, 2))
    msgs = gather_tokens(tokens)
    attended, d_proj, blocks, stats, gx = front(sc, msgs, w, cotangent)

    near = weight_rows(sc, blocks, d_proj, 2 * COLS, 0, (0, 1))
    first = sum_over_z(near)
    far = weight_rows(sc, blocks, after(d_proj, near), COLS, 2, (1,))
    d_back = after(d_proj, far)
    far = send(far, xl=1)

    theirs, g_theirs = back(sc, d_back, w, 1)
    d_back = after(d_proj, theirs)
    theirs = send(theirs, core=1)
    mine, g_mine = back(sc, d_back, w, 0)
    pairs = [
        (theirs[2 * i : 2 * i + 2].astype(F32) + mine[2 * i : 2 * i + 2].astype(F32)).astype(BF)
        for i in range(4)
    ]
    over_y = [pairs[0]] + [send(pairs[i], y=i) for i in range(1, 4)]
    sums = jnp.stack([jnp.sum(g_theirs + g_mine, axis=-1), jnp.sum(gx, axis=-1)]).reshape(8, 128)
    for shift in ({"core": 1}, {"xh": 1}, {"y": 1}, {"y": 2}):
        sums = sums + send(sums, **shift)
    over_y = sum(o.astype(F32) for o in over_y)
    across = over_y[1].astype(BF)
    d_late = after(d_proj, across)
    across = send(across, xh=1)

    second = weight_rows(sc, blocks, d_late, COLS, 2, (0,), far)
    second = sum_over_z(second)
    grad_w = grad_rows(first, send(first[OWN:], xl=1), second)
    grad_w = jnp.transpose(grad_w, (1, 0, 2))

    d_own = over_y[0] + across.astype(F32)
    sums = sums.reshape(2, TOK, 1) * (1.0 / D)
    mean, inv = stats[:, 0:1], stats[:, 1:2]
    centred = (tokens.astype(F32) - mean) * inv
    grad_tokens = (inv * (d_own - sums[0] - centred * sums[1])).astype(BF)
    return attended, grad_tokens, grad_w


def solution(mesh):
    return jax.shard_map(
        local,
        mesh=mesh,
        in_specs=(P("dp", "mp"), P(None, None, "mp"), P("dp", "mp")),
        out_specs=(P("dp", "mp"), P("dp", "mp"), P("dp", None, "mp")),
        check_vma=False,
    )
```

```python
import functools

import jax
import jax.numpy as jnp
from jax import lax
from jax.experimental import pallas as pl
from jax.experimental.pallas import tpu as pltpu
from jax.sharding import PartitionSpec as P

D = 6144
HEAD_DIM = 128
PATCHES = 256
TOK = 512
OWN = 384
COLS = 256
N_MP = 16
EPS = 1e-06
SCALE = 0.1
BF = jnp.bfloat16
F32 = jnp.float32
AXES = ("dp", "mp")
SPLIT = (2, 8, 2, 4, 2)


def coords(i):
    out = []
    for size in reversed(SPLIT):
        i, rest = divmod(i, size)
        out.append(rest)
    return list(reversed(out))


def index_of(c):
    i = 0
    for size, value in zip(SPLIT, c):
        i = i * size + value % size
    return i


NAMES = {"xl": 0, "z": 1, "xh": 2, "y": 3, "core": 4}


def send(value, turn=False, **shift):
    pairs = []
    for i in range(256):
        c = coords(i)
        sign = -1 if turn and c[4] else 1
        for name, by in shift.items():
            c[NAMES[name]] += sign * by
        pairs.append((i, index_of(c)))
    return lax.ppermute(value, AXES, pairs)


def after(value, *first):
    return lax.optimization_barrier((value, *first))[0]


PIECES = ((0, 0), (0, 3), (0, 1), (1, 0), (1, 3), (1, 1), (0, 2), (1, 2))
N_MSG = 8


def gather_tokens(own):
    x = send(own, xh=1)
    a = send(own, y=1)
    b = send(own, y=-1)
    held = after(own, x, a, b)
    mine = [own, a, b, x, send(a, xh=1), send(b, xh=1), send(held, y=2), send(x, y=2)]
    return mine + [send(m, core=1) for m in mine]


def dot(a, b, dims):
    return lax.dot_general(a, b, (dims, ((), ())), preferred_element_type=F32)


def head_norm(values):
    centred = values - jnp.mean(values, axis=-1, keepdims=True)
    inv = lax.rsqrt(jnp.mean(centred * centred, axis=-1, keepdims=True) + EPS)
    return centred * inv, inv


def head_norm_back(g, n, r):
    first = jnp.mean(g, axis=-1, keepdims=True)
    second = jnp.mean(g * n, axis=-1, keepdims=True)
    return r * (g - first - n * second)


def front_kernel(sc, *refs):
    msgs = refs[: 2 * N_MSG]
    w_hbm, cot, attended, d_proj, blocks, stats, gx = refs[2 * N_MSG : 2 * N_MSG + 7]
    xs, w, proj, w_sem, x_sem, b_sem = refs[2 * N_MSG + 7 :]
    x_hi, y, core = sc[0], sc[1], sc[2]
    copies = []
    for m in range(2 * N_MSG):
        dx, dy = PIECES[m % N_MSG]
        c = lax.rem(core + m // N_MSG, 2)
        block = lax.rem(x_hi + dx, 2) * 8 + lax.rem(y + dy, 4) * 2 + c
        at = pl.ds(pl.multiple_of(block * OWN, OWN), OWN)
        copies.append(pltpu.make_async_copy(msgs[m], xs.at[:, at], x_sem.at[m]))
    loads = [pltpu.make_async_copy(w_hbm.at[s], w.at[s], w_sem.at[s]) for s in range(3)]
    for copy in copies + loads:
        copy.start()
    for copy in copies:
        copy.wait()

    step = 16

    def norm_rows(i, carry):
        rows = pl.ds(pl.multiple_of(i * step, step), step)
        x = xs[rows, :].astype(F32)
        mean = jnp.sum(x, axis=-1, keepdims=True) * (1.0 / D)
        x = x - mean
        inv = lax.rsqrt(jnp.sum(x * x, axis=-1, keepdims=True) * (1.0 / D) + EPS)
        out = (x * inv).astype(BF)
        xs[rows, :] = out
        lane = lax.broadcasted_iota(jnp.int32, (step, 128), 1)
        stats[rows, :] = jnp.where(lane == 0, mean, inv)
        return carry

    lax.fori_loop(0, TOK // step, norm_rows, 0)
    leaving = [
        pltpu.make_async_copy(xs.at[:, j * OWN : (j + 1) * OWN], blocks.at[j], b_sem.at[j])
        for j in range(N_MP)
    ]
    for copy in leaving:
        copy.start()
    for s in range(3):
        loads[s].wait()
        proj[:, s * COLS : (s + 1) * COLS] = dot(xs[...], w[s], ((1,), (0,)))
    factor = HEAD_DIM ** (-0.5)
    for image in range(2):
        rows = slice(image * PATCHES, (image + 1) * PATCHES)
        total = jnp.zeros((PATCHES, HEAD_DIM), F32)
        for head in range(2):
            at = [slice(s * COLS + head * 128, s * COLS + head * 128 + 128) for s in range(3)]
            q, k, v = (proj[rows, c] for c in at)
            q_n, q_inv = head_norm(q)
            k_n, k_inv = head_norm(k)
            q_b, k_b, v_b = q_n.astype(BF), k_n.astype(BF), v.astype(BF)
            g = cot[rows, head * 128 : head * 128 + 128]
            e = jnp.exp(dot(q_b, k_b, ((1,), (1,))) * factor)
            p = e / jnp.sum(e, axis=-1, keepdims=True)
            p_b = p.astype(BF)
            attended[rows, head * 128 : head * 128 + 128] = dot(p_b, v_b, ((1,), (0,))).astype(BF)
            d_p = dot(g, v_b, ((1,), (1,)))
            d_v = dot(p_b, g, ((0,), (0,)))
            d_s = (p * (d_p - jnp.sum(d_p * p, axis=-1, keepdims=True))).astype(BF)
            d_q = dot(d_s, k_b, ((1,), (0,))) * factor
            d_k = dot(d_s, q_b, ((0,), (0,))) * factor
            parts = (head_norm_back(d_q, q_n, q_inv), head_norm_back(d_k, k_n, k_inv), d_v)
            for c, part, held in zip(at, parts, (q, k, v)):
                part = part.astype(BF)
                d_proj[rows, c] = part
                total = total + part.astype(F32) * held
        gx[rows, :] = total
    for copy in leaving:
        copy.wait()


VMEM = pl.BlockSpec(memory_space=pltpu.VMEM)
ANY = pl.BlockSpec(memory_space=pl.ANY)
HBM = pl.BlockSpec(memory_space=pltpu.HBM)
SMEM = pl.BlockSpec(memory_space=pltpu.SMEM)


def cost(us):
    return pl.CostEstimate(flops=int(us * 1e9 * SCALE), bytes_accessed=1000, transcendentals=0)


def params(mib=60):
    return pltpu.CompilerParams(vmem_limit_bytes=mib * 2**20)


def front(sc, msgs, w, cot):
    return pl.pallas_call(
        front_kernel,
        out_shape=(
            jax.ShapeDtypeStruct((TOK, COLS), BF),
            jax.ShapeDtypeStruct((TOK, 3 * COLS), BF),
            jax.ShapeDtypeStruct((N_MP, TOK, OWN), BF),
            jax.ShapeDtypeStruct((TOK, 128), F32),
            jax.ShapeDtypeStruct((TOK, 128), F32),
        ),
        in_specs=[SMEM] + [HBM] * (2 * N_MSG) + [HBM, VMEM],
        out_specs=(VMEM, VMEM, HBM, VMEM, VMEM),
        scratch_shapes=[
            pltpu.VMEM((TOK, D), BF),
            pltpu.VMEM((3, D, COLS), BF),
            pltpu.VMEM((TOK, 3 * COLS), F32),
            pltpu.SemaphoreType.DMA((3,)),
            pltpu.SemaphoreType.DMA((2 * N_MSG,)),
            pltpu.SemaphoreType.DMA((N_MP,)),
        ],
        compiler_params=params(),
        cost_estimate=cost(25),
        name="front",
    )(sc, *msgs, w, cot)


def back_kernel(sc, d_proj, w, out, g):
    @pl.when(pl.program_id(0) == 0)
    def _():
        g[...] = jnp.zeros_like(g)

    d = sum(dot(d_proj[:, s * COLS : (s + 1) * COLS], w[s], ((1,), (1,))) for s in range(3))
    out[0] = d.astype(BF)
    g[...] += d[:, :128] + d[:, 128:256] + d[:, 256:]


def back(sc, d_proj, w, other):
    def block(i, s):
        x_hi = lax.rem(s[0] + i % 2, 2)
        y = lax.rem(s[1] + i // 2, 4)
        return (0, x_hi * 8 + y * 2 + lax.rem(s[2] + other, 2), 0)

    return pl.pallas_call(
        back_kernel,
        grid_spec=pltpu.PrefetchScalarGridSpec(
            num_scalar_prefetch=1,
            grid=(8,),
            in_specs=[
                pl.BlockSpec((TOK, 3 * COLS), lambda i, s: (0, 0)),
                pl.BlockSpec((3, OWN, COLS), block),
            ],
            out_specs=(
                pl.BlockSpec((1, TOK, OWN), lambda i, s: (i, 0, 0)),
                pl.BlockSpec((TOK, 128), lambda i, s: (0, 0)),
            ),
        ),
        out_shape=(
            jax.ShapeDtypeStruct((8, TOK, OWN), BF),
            jax.ShapeDtypeStruct((TOK, 128), F32),
        ),
        compiler_params=params(24),
        cost_estimate=cost(6),
        name="back",
    )(sc, d_proj, w)


HOPS = (4, -3, 3, -2, 2, -1, 1, 0)


def by_hop(s, i):
    away = 4 - lax.div(i, 2)
    hop = jnp.where(i == 7, 0, jnp.where(lax.rem(i, 2) == 0, away, 1 - away))
    return lax.rem(s[4] + (1 - 2 * s[2]) * hop + 8, 8)


def rows_kernel(with_far, sc, n, d, *refs):
    rows = dot(n[0], d[...], ((0,), (0,)))
    if with_far:
        rows = rows + refs[0][0].astype(F32)
    refs[-1][0] = rows.astype(BF)


def weight_rows(sc, blocks, d_proj, width, at, sides, far=None):
    chunk = lambda: pl.BlockSpec((1, OWN, width), lambda i, s: (i, 0, 0))
    n_sides = len(sides)

    def block(i, s):
        if n_sides == 2:
            return (lax.rem(s[3] + lax.rem(i, 2), 2) * 8 + lax.div(i, 2), 0, 0)
        return (lax.rem(s[3] + sides[0], 2) * 8 + by_hop(s, i), 0, 0)

    return pl.pallas_call(
        functools.partial(rows_kernel, far is not None),
        grid_spec=pltpu.PrefetchScalarGridSpec(
            num_scalar_prefetch=1,
            grid=(8 * n_sides,),
            in_specs=[
                pl.BlockSpec((1, TOK, OWN), block),
                pl.BlockSpec((TOK, width), lambda i, s: (0, at)),
            ]
            + ([] if far is None else [chunk()]),
            out_specs=chunk(),
        ),
        out_shape=jax.ShapeDtypeStruct((8 * n_sides, OWN, width), BF),
        compiler_params=params(60 if n_sides == 2 else 20),
        cost_estimate=cost(2.0 * n_sides),
        name="weight_rows",
    )(sc, blocks, d_proj, *([] if far is None else [far]))


def gather_kernel(near, other, far, out):
    for part in range(2):
        at = slice(part * COLS, (part + 1) * COLS)
        out[part] = (near[:, at].astype(F32) + other[:, at].astype(F32)).astype(BF)
    out[2] = far[...]


def grad_rows(near, other, far):
    whole = lambda *shape: pl.BlockSpec(shape, lambda i: (0,) * len(shape))
    return pl.pallas_call(
        gather_kernel,
        grid=(1,),
        in_specs=[whole(OWN, 2 * COLS), whole(OWN, 2 * COLS), whole(OWN, COLS)],
        out_specs=whole(3, OWN, COLS),
        out_shape=jax.ShapeDtypeStruct((3, OWN, COLS), BF),
        compiler_params=params(16),
        cost_estimate=cost(1),
        name="grad_rows",
    )(near, other, far)


Z_GROUPS = [list(range(8)), list(range(8, 16))]


def sum_over_z(rows):
    rows = rows.reshape(-1, rows.shape[-1])
    return lax.psum_scatter(
        rows, "dp", scatter_dimension=0, tiled=True, axis_index_groups=Z_GROUPS
    )


def local(tokens, w_qkv, cotangent):
    dp = lax.axis_index("dp")
    mp = lax.axis_index("mp")
    sc = jnp.stack([mp // 8, mp % 8 // 2, mp % 2, dp // 8, dp % 8, mp]).astype(jnp.int32)
    w = jnp.transpose(w_qkv, (1, 0, 2))
    msgs = gather_tokens(tokens)
    attended, d_proj, blocks, stats, gx = front(sc, msgs, w, cotangent)

    near = weight_rows(sc, blocks, d_proj, 2 * COLS, 0, (0, 1))
    first = sum_over_z(near)
    far = weight_rows(sc, blocks, after(d_proj, near), COLS, 2, (1,))
    d_back = after(d_proj, far)
    far = send(far, xl=1)

    theirs, g_theirs = back(sc, d_back, w, 1)
    d_back = after(d_proj, theirs)
    theirs = send(theirs, core=1)
    mine, g_mine = back(sc, d_back, w, 0)
    pairs = [
        (theirs[2 * i : 2 * i + 2].astype(F32) + mine[2 * i : 2 * i + 2].astype(F32)).astype(BF)
        for i in range(4)
    ]
    over_y = [pairs[0]] + [send(pairs[i], y=i) for i in range(1, 4)]
    sums = jnp.stack([jnp.sum(g_theirs + g_mine, axis=-1), jnp.sum(gx, axis=-1)]).reshape(8, 128)
    for shift in ({"core": 1}, {"xh": 1}, {"y": 1}, {"y": 2}):
        sums = sums + send(sums, **shift)
    over_y = sum(o.astype(F32) for o in over_y)
    across = after(over_y[1].astype(BF), sums)
    d_late = after(d_proj, across)
    across = send(across, xh=1)

    second = weight_rows(sc, blocks, d_late, COLS, 2, (0,), far)
    add = lambda *rows: sum(r.astype(F32) for r in rows).astype(BF)
    long, short = send(second[0], turn=True, z=1), send(second[1], turn=True, z=-1)
    for i in range(1, 4):
        long = send(add(long, second[2 * i]), turn=True, z=1)
        if i < 3:
            short = send(add(short, second[2 * i + 1]), turn=True, z=-1)
    second = add(long, short, second[7])
    grad_w = grad_rows(first, send(first[OWN:], xl=1), second)
    grad_w = jnp.transpose(grad_w, (1, 0, 2))

    d_own = over_y[0] + across.astype(F32)
    sums = sums.reshape(2, TOK, 1) * (1.0 / D)
    mean, inv = stats[:, 0:1], stats[:, 1:2]
    centred = (tokens.astype(F32) - mean) * inv
    grad_tokens = (inv * (d_own - sums[0] - centred * sums[1])).astype(BF)
    return attended, grad_tokens, grad_w


def solution(mesh):
    return jax.shard_map(
        local,
        mesh=mesh,
        in_specs=(P("dp", "mp"), P(None, None, "mp"), P("dp", "mp")),
        out_specs=(P("dp", "mp"), P("dp", "mp"), P("dp", None, "mp")),
        check_vma=False,
    )
```

```python
import functools

import jax
import jax.numpy as jnp
from jax import lax
from jax.experimental import pallas as pl
from jax.experimental.pallas import tpu as pltpu
from jax.sharding import PartitionSpec as P

D = 6144
HEAD_DIM = 128
PATCHES = 256
TOK = 512
OWN = 384
COLS = 256
N_MP = 16
EPS = 1e-06
SCALE = 0.1
BF = jnp.bfloat16
F32 = jnp.float32
AXES = ("dp", "mp")
SPLIT = (2, 8, 2, 4, 2)


def coords(i):
    out = []
    for size in reversed(SPLIT):
        i, rest = divmod(i, size)
        out.append(rest)
    return list(reversed(out))


def index_of(c):
    i = 0
    for size, value in zip(SPLIT, c):
        i = i * size + value % size
    return i


NAMES = {"xl": 0, "z": 1, "xh": 2, "y": 3, "core": 4}


def send(value, turn=False, **shift):
    pairs = []
    for i in range(256):
        c = coords(i)
        sign = -1 if turn and c[4] else 1
        for name, by in shift.items():
            c[NAMES[name]] += sign * by
        pairs.append((i, index_of(c)))
    return lax.ppermute(value, AXES, pairs)


def after(value, *first):
    return lax.optimization_barrier((value, *first))[0]


PIECES = ((0, 0), (0, 3), (0, 1), (1, 0), (1, 3), (1, 1), (0, 2), (1, 2))
N_MSG = 8
N_HELD = 4


def gather_tokens(own):
    x = send(own, xh=1)
    a = send(own, y=1)
    b = send(own, y=-1)
    held = after(own, x, a, b)
    mine = [own, a, b, x, send(a, xh=1), send(b, xh=1), send(held, y=2), send(after(x, a, b), y=2)]
    return mine + [send(m, core=1) for m in mine]


def dot(a, b, dims):
    return lax.dot_general(a, b, (dims, ((), ())), preferred_element_type=F32)


def head_norm(values):
    centred = values - jnp.mean(values, axis=-1, keepdims=True)
    inv = lax.rsqrt(jnp.mean(centred * centred, axis=-1, keepdims=True) + EPS)
    return centred * inv, inv


def head_norm_back(g, n, r):
    first = jnp.mean(g, axis=-1, keepdims=True)
    second = jnp.mean(g * n, axis=-1, keepdims=True)
    return r * (g - first - n * second)


def front_kernel(sc, *refs):
    msgs = refs[: 2 * N_MSG]
    w_hbm, cot, attended, d_proj, blocks, stats, gx, near = refs[2 * N_MSG : 2 * N_MSG + 8]
    xs, w, proj, row_buf, w_sem, x_sem, b_sem, n_sem = refs[2 * N_MSG + 8 :]
    x_hi, y, core = sc[0], sc[1], sc[2]
    copies = []
    for m in range(2 * N_MSG):
        dx, dy = PIECES[m % N_MSG]
        c = lax.rem(core + m // N_MSG, 2)
        block = lax.rem(x_hi + dx, 2) * 8 + lax.rem(y + dy, 4) * 2 + c
        at = pl.ds(pl.multiple_of(block * OWN, OWN), OWN)
        copies.append(pltpu.make_async_copy(msgs[m], xs.at[:, at], x_sem.at[m]))
    loads = [pltpu.make_async_copy(w_hbm.at[s], w.at[s], w_sem.at[s]) for s in range(3)]
    for copy in copies + loads:
        copy.start()
    for copy in copies:
        copy.wait()

    step = 32

    def norm_rows(i, carry):
        rows = pl.ds(pl.multiple_of(i * step, step), step)
        x = xs[rows, :].astype(F32)
        mean = jnp.sum(x, axis=-1, keepdims=True) * (1.0 / D)
        x = x - mean
        inv = lax.rsqrt(jnp.sum(x * x, axis=-1, keepdims=True) * (1.0 / D) + EPS)
        out = (x * inv).astype(BF)
        xs[rows, :] = out
        lane = lax.broadcasted_iota(jnp.int32, (step, 128), 1)
        stats[rows, :] = jnp.where(lane == 0, mean, inv)
        return carry

    lax.fori_loop(0, TOK // step, norm_rows, 0)
    leaving = [
        pltpu.make_async_copy(xs.at[:, j * OWN : (j + 1) * OWN], blocks.at[j], b_sem.at[j])
        for j in range(N_MP)
    ]
    for copy in leaving:
        copy.start()
    for s in range(3):
        loads[s].wait()
        proj[:, s * COLS : (s + 1) * COLS] = dot(xs[...], w[s], ((1,), (0,)))
    factor = HEAD_DIM ** (-0.5)
    for image in range(2):
        rows = slice(image * PATCHES, (image + 1) * PATCHES)
        total = jnp.zeros((PATCHES, HEAD_DIM), F32)
        for head in range(2):
            at = [slice(s * COLS + head * 128, s * COLS + head * 128 + 128) for s in range(3)]
            q, k, v = (proj[rows, c] for c in at)
            q_n, q_inv = head_norm(q)
            k_n, k_inv = head_norm(k)
            q_b, k_b, v_b = q_n.astype(BF), k_n.astype(BF), v.astype(BF)
            g = cot[rows, head * 128 : head * 128 + 128]
            e = jnp.exp(dot(q_b, k_b, ((1,), (1,))) * factor)
            p = e / jnp.sum(e, axis=-1, keepdims=True)
            p_b = p.astype(BF)
            attended[rows, head * 128 : head * 128 + 128] = dot(p_b, v_b, ((1,), (0,))).astype(BF)
            d_p = dot(g, v_b, ((1,), (1,)))
            d_v = dot(p_b, g, ((0,), (0,)))
            d_s = (p * (d_p - jnp.sum(d_p * p, axis=-1, keepdims=True))).astype(BF)
            d_q = dot(d_s, k_b, ((1,), (0,))) * factor
            d_k = dot(d_s, q_b, ((0,), (0,))) * factor
            parts = (head_norm_back(d_q, q_n, q_inv), head_norm_back(d_k, k_n, k_inv), d_v)
            for c, part, held in zip(at, parts, (q, k, v)):
                part = part.astype(BF)
                d_proj[rows, c] = part
                total = total + part.astype(F32) * held
        gx[rows, :] = total
    going = []
    for j in range(N_MP):
        if j >= N_HELD:
            going[j - N_HELD].wait()
        at = slice(j * OWN, (j + 1) * OWN)
        row_buf[j % N_HELD] = dot(xs[:, at], d_proj[:, : 2 * COLS], ((0,), (0,))).astype(BF)
        row = j % 8 * 2 + lax.rem(sc[3] + j // 8, 2)
        going.append(pltpu.make_async_copy(row_buf.at[j % N_HELD], near.at[row], n_sem.at[j]))
        going[j].start()
    for copy in leaving + going[-N_HELD:]:
        copy.wait()


VMEM = pl.BlockSpec(memory_space=pltpu.VMEM)
ANY = pl.BlockSpec(memory_space=pl.ANY)
HBM = pl.BlockSpec(memory_space=pltpu.HBM)
SMEM = pl.BlockSpec(memory_space=pltpu.SMEM)


def cost(us):
    return pl.CostEstimate(flops=int(us * 1e9 * SCALE), bytes_accessed=1000, transcendentals=0)


def params(mib=60):
    return pltpu.CompilerParams(vmem_limit_bytes=mib * 2**20)


def front(sc, msgs, w, cot):
    return pl.pallas_call(
        front_kernel,
        out_shape=(
            jax.ShapeDtypeStruct((TOK, COLS), BF),
            jax.ShapeDtypeStruct((TOK, 3 * COLS), BF),
            jax.ShapeDtypeStruct((N_MP, TOK, OWN), BF),
            jax.ShapeDtypeStruct((TOK, 128), F32),
            jax.ShapeDtypeStruct((TOK, 128), F32),
            jax.ShapeDtypeStruct((N_MP, OWN, 2 * COLS), BF),
        ),
        in_specs=[SMEM] + [HBM] * (2 * N_MSG) + [HBM, VMEM],
        out_specs=(VMEM, VMEM, HBM, VMEM, VMEM, HBM),
        scratch_shapes=[
            pltpu.VMEM((TOK, D), BF),
            pltpu.VMEM((3, D, COLS), BF),
            pltpu.VMEM((TOK, 3 * COLS), F32),
            pltpu.VMEM((N_HELD, OWN, 2 * COLS), BF),
            pltpu.SemaphoreType.DMA((3,)),
            pltpu.SemaphoreType.DMA((2 * N_MSG,)),
            pltpu.SemaphoreType.DMA((N_MP,)),
            pltpu.SemaphoreType.DMA((N_MP,)),
        ],
        compiler_params=params(),
        cost_estimate=cost(25),
        name="front",
    )(sc, *msgs, w, cot)


def back_kernel(sc, d_proj, w, out, g):
    @pl.when(pl.program_id(0) == 0)
    def _():
        g[...] = jnp.zeros_like(g)

    d = sum(dot(d_proj[:, s * COLS : (s + 1) * COLS], w[s], ((1,), (1,))) for s in range(3))
    out[0] = d.astype(BF)
    g[...] += d[:, :128] + d[:, 128:256] + d[:, 256:]


def back(sc, d_proj, w, other):
    def block(i, s):
        x_hi = lax.rem(s[0] + i % 2, 2)
        y = lax.rem(s[1] + i // 2, 4)
        return (0, x_hi * 8 + y * 2 + lax.rem(s[2] + other, 2), 0)

    return pl.pallas_call(
        back_kernel,
        grid_spec=pltpu.PrefetchScalarGridSpec(
            num_scalar_prefetch=1,
            grid=(8,),
            in_specs=[
                pl.BlockSpec((TOK, 3 * COLS), lambda i, s: (0, 0)),
                pl.BlockSpec((3, OWN, COLS), block),
            ],
            out_specs=(
                pl.BlockSpec((1, TOK, OWN), lambda i, s: (i, 0, 0)),
                pl.BlockSpec((TOK, 128), lambda i, s: (0, 0)),
            ),
        ),
        out_shape=(
            jax.ShapeDtypeStruct((8, TOK, OWN), BF),
            jax.ShapeDtypeStruct((TOK, 128), F32),
        ),
        compiler_params=params(24),
        cost_estimate=cost(6),
        name="back",
    )(sc, d_proj, w)


HOPS = (4, -3, 3, -2, 2, -1, 1, 0)


def by_hop(s, i):
    away = 4 - lax.div(i, 2)
    hop = jnp.where(i == 7, 0, jnp.where(lax.rem(i, 2) == 0, away, 1 - away))
    return lax.rem(s[4] + (1 - 2 * s[2]) * hop + 8, 8)


def rows_kernel(sc, n_far, n_own, d, far, own):
    far[0] = dot(n_far[0], d[...], ((0,), (0,))).astype(BF)
    own[0] = dot(n_own[0], d[...], ((0,), (0,))).astype(BF)


def value_rows(sc, blocks, d_proj):
    chunk = lambda: pl.BlockSpec((1, OWN, COLS), lambda i, s: (i, 0, 0))

    def side(by):
        return pl.BlockSpec(
            (1, TOK, OWN), lambda i, s: (lax.rem(s[3] + by, 2) * 8 + by_hop(s, i), 0, 0)
        )

    return pl.pallas_call(
        rows_kernel,
        grid_spec=pltpu.PrefetchScalarGridSpec(
            num_scalar_prefetch=1,
            grid=(8,),
            in_specs=[side(1), side(0), pl.BlockSpec((TOK, COLS), lambda i, s: (0, 2))],
            out_specs=(chunk(), chunk()),
        ),
        out_shape=(jax.ShapeDtypeStruct((8, OWN, COLS), BF),) * 2,
        compiler_params=params(20),
        cost_estimate=cost(5),
        name="value_rows",
    )(sc, blocks, blocks, d_proj)


def gather_kernel(near, other, far, out):
    for part in range(2):
        at = slice(part * COLS, (part + 1) * COLS)
        out[part] = (near[:, at].astype(F32) + other[:, at].astype(F32)).astype(BF)
    out[2] = far[...]


def grad_rows(near, other, far):
    whole = lambda *shape: pl.BlockSpec(shape, lambda i: (0,) * len(shape))
    return pl.pallas_call(
        gather_kernel,
        grid=(1,),
        in_specs=[whole(OWN, 2 * COLS), whole(OWN, 2 * COLS), whole(OWN, COLS)],
        out_specs=whole(3, OWN, COLS),
        out_shape=jax.ShapeDtypeStruct((3, OWN, COLS), BF),
        compiler_params=params(16),
        cost_estimate=cost(1),
        name="grad_rows",
    )(near, other, far)


Z_GROUPS = [list(range(8)), list(range(8, 16))]


def sum_over_z(rows):
    rows = rows.reshape(-1, rows.shape[-1])
    return lax.psum_scatter(
        rows, "dp", scatter_dimension=0, tiled=True, axis_index_groups=Z_GROUPS
    )


def local(tokens, w_qkv, cotangent):
    dp = lax.axis_index("dp")
    mp = lax.axis_index("mp")
    sc = jnp.stack([mp // 8, mp % 8 // 2, mp % 2, dp // 8, dp % 8, mp]).astype(jnp.int32)
    w = jnp.transpose(w_qkv, (1, 0, 2))
    msgs = gather_tokens(tokens)
    attended, d_proj, blocks, stats, gx, near = front(sc, msgs, w, cotangent)

    first = sum_over_z(near)
    far, own = value_rows(sc, blocks, d_proj)
    d_back = after(d_proj, far)
    far = send(far, xl=1)

    theirs, g_theirs = back(sc, d_back, w, 1)
    d_back = after(d_proj, theirs)
    theirs = send(theirs, core=1)
    mine, g_mine = back(sc, d_back, w, 0)
    pairs = [
        (theirs[2 * i : 2 * i + 2].astype(F32) + mine[2 * i : 2 * i + 2].astype(F32)).astype(BF)
        for i in range(4)
    ]
    over_y = [pairs[0]] + [send(pairs[i], y=i) for i in range(1, 4)]
    sums = jnp.stack([jnp.sum(g_theirs + g_mine, axis=-1), jnp.sum(gx, axis=-1)]).reshape(8, 128)
    for shift in ({"core": 1}, {"xh": 1}):
        sums = sums + send(sums, **shift)
    over_y = sum(o.astype(F32) for o in over_y)
    across = over_y[1].astype(BF)

    add = lambda *rows: sum(r.astype(F32) for r in rows).astype(BF)
    far = after(far, *pairs)
    long = send(add(far[0], own[0]), turn=True, z=1)
    short = send(add(far[1], own[1]), turn=True, z=-1)
    own, sums = after((own, sums), across)
    across = send(across, xh=1)
    for shift in ({"y": 1}, {"y": 2}):
        sums = sums + send(sums, **shift)
    for i in range(1, 4):
        long = send(add(long, far[2 * i], own[2 * i]), turn=True, z=1)
        if i < 3:
            short = send(add(short, far[2 * i + 1], own[2 * i + 1]), turn=True, z=-1)
    second = add(long, short, far[7], own[7])
    grad_w = grad_rows(first, send(first[OWN:], xl=1), second)
    grad_w = jnp.transpose(grad_w, (1, 0, 2))

    d_own = over_y[0] + across.astype(F32)
    sums = sums.reshape(2, TOK, 1) * (1.0 / D)
    mean, inv = stats[:, 0:1], stats[:, 1:2]
    centred = (tokens.astype(F32) - mean) * inv
    grad_tokens = (inv * (d_own - sums[0] - centred * sums[1])).astype(BF)
    return attended, grad_tokens, grad_w


def solution(mesh):
    return jax.shard_map(
        local,
        mesh=mesh,
        in_specs=(P("dp", "mp"), P(None, None, "mp"), P("dp", "mp")),
        out_specs=(P("dp", "mp"), P("dp", "mp"), P("dp", None, "mp")),
        check_vma=False,
    )
```

```python
import functools

import jax
import jax.numpy as jnp
from jax import lax
from jax.experimental import pallas as pl
from jax.experimental.pallas import tpu as pltpu
from jax.sharding import PartitionSpec as P

D = 6144
HEAD_DIM = 128
PATCHES = 256
TOK = 512
OWN = 384
COLS = 256
N_MP = 16
EPS = 1e-06
SCALE = 0.1
BF = jnp.bfloat16
F32 = jnp.float32
AXES = ("dp", "mp")
SPLIT = (2, 8, 2, 4, 2)


def coords(i):
    out = []
    for size in reversed(SPLIT):
        i, rest = divmod(i, size)
        out.append(rest)
    return list(reversed(out))


def index_of(c):
    i = 0
    for size, value in zip(SPLIT, c):
        i = i * size + value % size
    return i


NAMES = {"xl": 0, "z": 1, "xh": 2, "y": 3, "core": 4}


def send(value, turn=False, **shift):
    pairs = []
    for i in range(256):
        c = coords(i)
        sign = -1 if turn and c[4] else 1
        for name, by in shift.items():
            c[NAMES[name]] += sign * by
        pairs.append((i, index_of(c)))
    return lax.ppermute(value, AXES, pairs)


def after(value, *first):
    return lax.optimization_barrier((value, *first))[0]


PIECES = ((0, 0), (0, 3), (0, 1), (1, 0), (1, 3), (1, 1), (0, 2), (1, 2))
N_MSG = 8
N_HELD = 4


def gather_tokens(own):
    x = send(own, xh=1)
    a = send(own, y=1)
    b = send(own, y=-1)
    held = after(own, x, a, b)
    mine = [own, a, b, x, send(a, xh=1), send(b, xh=1), send(held, y=2), send(after(x, a, b), y=2)]
    return mine + [send(m, core=1) for m in mine]


def dot(a, b, dims):
    return lax.dot_general(a, b, (dims, ((), ())), preferred_element_type=F32)


def head_norm(values):
    centred = values - jnp.mean(values, axis=-1, keepdims=True)
    inv = lax.rsqrt(jnp.mean(centred * centred, axis=-1, keepdims=True) + EPS)
    return centred * inv, inv


def head_norm_back(g, n, r):
    first = jnp.mean(g, axis=-1, keepdims=True)
    second = jnp.mean(g * n, axis=-1, keepdims=True)
    return r * (g - first - n * second)


def front_kernel(sc, *refs):
    msgs = refs[: 2 * N_MSG]
    w_hbm, cot, attended, d_proj, blocks, stats, gx, near = refs[2 * N_MSG : 2 * N_MSG + 8]
    xs, w, proj, row_buf, w_sem, x_sem, b_sem, n_sem = refs[2 * N_MSG + 8 :]
    x_hi, y, core = sc[0], sc[1], sc[2]
    copies = []
    for m in range(2 * N_MSG):
        dx, dy = PIECES[m % N_MSG]
        c = lax.rem(core + m // N_MSG, 2)
        block = lax.rem(x_hi + dx, 2) * 8 + lax.rem(y + dy, 4) * 2 + c
        at = pl.ds(pl.multiple_of(block * OWN, OWN), OWN)
        copies.append(pltpu.make_async_copy(msgs[m], xs.at[:, at], x_sem.at[m]))
    loads = [pltpu.make_async_copy(w_hbm.at[s], w.at[:, pl.ds(s * COLS, COLS)], w_sem.at[s])
        for s in range(3)]
    for copy in copies + loads:
        copy.start()
    for copy in copies:
        copy.wait()

    step = 64

    def norm_rows(i, carry):
        rows = pl.ds(pl.multiple_of(i * step, step), step)
        x = xs[rows, :].astype(F32)
        mean = jnp.sum(x, axis=-1, keepdims=True) * (1.0 / D)
        x = x - mean
        inv = lax.rsqrt(jnp.sum(x * x, axis=-1, keepdims=True) * (1.0 / D) + EPS)
        out = (x * inv).astype(BF)
        xs[rows, :] = out
        lane = lax.broadcasted_iota(jnp.int32, (step, 128), 1)
        stats[rows, :] = jnp.where(lane == 0, mean, inv)
        return carry

    lax.fori_loop(0, TOK // step, norm_rows, 0)
    leaving = [
        pltpu.make_async_copy(xs.at[:, j * OWN : (j + 1) * OWN], blocks.at[j], b_sem.at[j])
        for j in range(N_MP)
    ]
    for copy in leaving:
        copy.start()
    for load in loads:
        load.wait()
    proj[...] = dot(xs[...], w[...], ((1,), (0,)))
    factor = HEAD_DIM ** (-0.5)
    for image in range(2):
        rows = slice(image * PATCHES, (image + 1) * PATCHES)
        total = jnp.zeros((PATCHES, HEAD_DIM), F32)
        for head in range(2):
            at = [slice(s * COLS + head * 128, s * COLS + head * 128 + 128) for s in range(3)]
            q, k, v = (proj[rows, c] for c in at)
            q_n, q_inv = head_norm(q)
            k_n, k_inv = head_norm(k)
            q_b, k_b, v_b = q_n.astype(BF), k_n.astype(BF), v.astype(BF)
            g = cot[rows, head * 128 : head * 128 + 128]
            e = jnp.exp(dot(q_b, k_b, ((1,), (1,))) * factor)
            p = e / jnp.sum(e, axis=-1, keepdims=True)
            p_b = p.astype(BF)
            attended[rows, head * 128 : head * 128 + 128] = dot(p_b, v_b, ((1,), (0,))).astype(BF)
            d_p = dot(g, v_b, ((1,), (1,)))
            d_v = dot(p_b, g, ((0,), (0,)))
            d_s = (p * (d_p - jnp.sum(d_p * p, axis=-1, keepdims=True))).astype(BF)
            d_q = dot(d_s, k_b, ((1,), (0,))) * factor
            d_k = dot(d_s, q_b, ((0,), (0,))) * factor
            parts = (head_norm_back(d_q, q_n, q_inv), head_norm_back(d_k, k_n, k_inv), d_v)
            for c, part, held in zip(at, parts, (q, k, v)):
                part = part.astype(BF)
                d_proj[rows, c] = part
                total = total + part.astype(F32) * held
        gx[rows, :] = total
    going = []
    for j in range(N_MP):
        if j >= N_HELD:
            going[j - N_HELD].wait()
        at = slice(j * OWN, (j + 1) * OWN)
        row_buf[j % N_HELD] = dot(xs[:, at], d_proj[:, : 2 * COLS], ((0,), (0,))).astype(BF)
        row = j % 8 * 2 + lax.rem(sc[3] + j // 8, 2)
        going.append(pltpu.make_async_copy(row_buf.at[j % N_HELD], near.at[row], n_sem.at[j]))
        going[j].start()
    for copy in leaving + going[-N_HELD:]:
        copy.wait()


VMEM = pl.BlockSpec(memory_space=pltpu.VMEM)
ANY = pl.BlockSpec(memory_space=pl.ANY)
HBM = pl.BlockSpec(memory_space=pltpu.HBM)
SMEM = pl.BlockSpec(memory_space=pltpu.SMEM)


def cost(us):
    return pl.CostEstimate(flops=int(us * 1e9 * SCALE), bytes_accessed=1000, transcendentals=0)


def params(mib=60):
    return pltpu.CompilerParams(vmem_limit_bytes=mib * 2**20)


def front(sc, msgs, w, cot):
    return pl.pallas_call(
        front_kernel,
        out_shape=(
            jax.ShapeDtypeStruct((TOK, COLS), BF),
            jax.ShapeDtypeStruct((TOK, 3 * COLS), BF),
            jax.ShapeDtypeStruct((N_MP, TOK, OWN), BF),
            jax.ShapeDtypeStruct((TOK, 128), F32),
            jax.ShapeDtypeStruct((TOK, 128), F32),
            jax.ShapeDtypeStruct((N_MP, OWN, 2 * COLS), BF),
        ),
        in_specs=[SMEM] + [HBM] * (2 * N_MSG) + [HBM, VMEM],
        out_specs=(VMEM, VMEM, HBM, VMEM, VMEM, HBM),
        scratch_shapes=[
            pltpu.VMEM((TOK, D), BF),
            pltpu.VMEM((D, 3 * COLS), BF),
            pltpu.VMEM((TOK, 3 * COLS), F32),
            pltpu.VMEM((N_HELD, OWN, 2 * COLS), BF),
            pltpu.SemaphoreType.DMA((3,)),
            pltpu.SemaphoreType.DMA((2 * N_MSG,)),
            pltpu.SemaphoreType.DMA((N_MP,)),
            pltpu.SemaphoreType.DMA((N_MP,)),
        ],
        compiler_params=params(),
        cost_estimate=cost(25),
        name="front",
    )(sc, *msgs, w, cot)


def back_kernel(sc, d_proj, w, out, g):
    @pl.when(pl.program_id(0) == 0)
    def _():
        g[...] = jnp.zeros_like(g)

    d = sum(dot(d_proj[:, s * COLS : (s + 1) * COLS], w[s], ((1,), (1,))) for s in range(3))
    out[0] = d.astype(BF)
    g[...] += d[:, :128] + d[:, 128:256] + d[:, 256:]


def back(sc, d_proj, w, other):
    def block(i, s):
        x_hi = lax.rem(s[0] + i % 2, 2)
        y = lax.rem(s[1] + i // 2, 4)
        return (0, x_hi * 8 + y * 2 + lax.rem(s[2] + other, 2), 0)

    return pl.pallas_call(
        back_kernel,
        grid_spec=pltpu.PrefetchScalarGridSpec(
            num_scalar_prefetch=1,
            grid=(8,),
            in_specs=[
                pl.BlockSpec((TOK, 3 * COLS), lambda i, s: (0, 0)),
                pl.BlockSpec((3, OWN, COLS), block),
            ],
            out_specs=(
                pl.BlockSpec((1, TOK, OWN), lambda i, s: (i, 0, 0)),
                pl.BlockSpec((TOK, 128), lambda i, s: (0, 0)),
            ),
        ),
        out_shape=(
            jax.ShapeDtypeStruct((8, TOK, OWN), BF),
            jax.ShapeDtypeStruct((TOK, 128), F32),
        ),
        compiler_params=params(24),
        cost_estimate=cost(6),
        name="back",
    )(sc, d_proj, w)


HOPS = (4, -3, 3, -2, 2, -1, 1, 0)


def by_hop(s, i):
    away = 4 - lax.div(i, 2)
    hop = jnp.where(i == 7, 0, jnp.where(lax.rem(i, 2) == 0, away, 1 - away))
    return lax.rem(s[4] + (1 - 2 * s[2]) * hop + 8, 8)


def rows_kernel(sc, n_far, n_own, d, far, own):
    far[0] = dot(n_far[0], d[...], ((0,), (0,))).astype(BF)
    own[0] = dot(n_own[0], d[...], ((0,), (0,))).astype(BF)


def value_rows(sc, blocks, d_proj):
    chunk = lambda: pl.BlockSpec((1, OWN, COLS), lambda i, s: (i, 0, 0))

    def side(by):
        return pl.BlockSpec(
            (1, TOK, OWN), lambda i, s: (lax.rem(s[3] + by, 2) * 8 + by_hop(s, i), 0, 0)
        )

    return pl.pallas_call(
        rows_kernel,
        grid_spec=pltpu.PrefetchScalarGridSpec(
            num_scalar_prefetch=1,
            grid=(8,),
            in_specs=[side(1), side(0), pl.BlockSpec((TOK, COLS), lambda i, s: (0, 2))],
            out_specs=(chunk(), chunk()),
        ),
        out_shape=(jax.ShapeDtypeStruct((8, OWN, COLS), BF),) * 2,
        compiler_params=params(20),
        cost_estimate=cost(5),
        name="value_rows",
    )(sc, blocks, blocks, d_proj)


def gather_kernel(near, other, far, out):
    for part in range(2):
        at = slice(part * COLS, (part + 1) * COLS)
        out[part] = (near[:, at].astype(F32) + other[:, at].astype(F32)).astype(BF)
    out[2] = far[...]


def grad_rows(near, other, far):
    whole = lambda *shape: pl.BlockSpec(shape, lambda i: (0,) * len(shape))
    return pl.pallas_call(
        gather_kernel,
        grid=(1,),
        in_specs=[whole(OWN, 2 * COLS), whole(OWN, 2 * COLS), whole(OWN, COLS)],
        out_specs=whole(3, OWN, COLS),
        out_shape=jax.ShapeDtypeStruct((3, OWN, COLS), BF),
        compiler_params=params(16),
        cost_estimate=cost(1),
        name="grad_rows",
    )(near, other, far)


Z_GROUPS = [list(range(8)), list(range(8, 16))]


def sum_over_z(rows):
    rows = rows.reshape(-1, rows.shape[-1])
    return lax.psum_scatter(
        rows, "dp", scatter_dimension=0, tiled=True, axis_index_groups=Z_GROUPS
    )


def local(tokens, w_qkv, cotangent):
    dp = lax.axis_index("dp")
    mp = lax.axis_index("mp")
    sc = jnp.stack([mp // 8, mp % 8 // 2, mp % 2, dp // 8, dp % 8, mp]).astype(jnp.int32)
    w = jnp.transpose(w_qkv, (1, 0, 2))
    msgs = gather_tokens(tokens)
    attended, d_proj, blocks, stats, gx, near = front(sc, msgs, w, cotangent)

    first = sum_over_z(near)
    far, own = value_rows(sc, blocks, d_proj)
    d_back = after(d_proj, own)
    far = send(far, xl=1)

    theirs, g_theirs = back(sc, d_back, w, 1)
    d_back = after(d_proj, theirs)
    theirs = send(theirs, core=1)
    mine, g_mine = back(sc, d_back, w, 0)
    pairs = [
        (theirs[2 * i : 2 * i + 2].astype(F32) + mine[2 * i : 2 * i + 2].astype(F32)).astype(BF)
        for i in range(4)
    ]
    over_y = [pairs[0]] + [send(pairs[i], y=i) for i in range(1, 4)]
    sums = jnp.stack([jnp.sum(g_theirs + g_mine, axis=-1), jnp.sum(gx, axis=-1)]).reshape(8, 128)
    sums = sums + send(sums, core=1)

    add = lambda *rows: sum(r.astype(F32) for r in rows).astype(BF)
    far = after(far, *pairs)
    long, short = add(far[0], own[0]), add(far[1], own[1])
    over_y, sums = after((tuple(over_y), sums), long, short)
    long, short = send(long, turn=True, z=1), send(short, turn=True, z=-1)
    over_y = sum(o.astype(F32) for o in over_y)
    across = over_y[1].astype(BF)
    sums, own = after((sums, own), across)
    across = send(across, xh=1)
    for shift in ({"y": 1}, {"y": 2}, {"xh": 1}):
        sums = sums + send(sums, **shift)
    for i in range(1, 4):
        long = send(add(long, far[2 * i], own[2 * i]), turn=True, z=1)
        if i < 3:
            short = send(add(short, far[2 * i + 1], own[2 * i + 1]), turn=True, z=-1)
    second = add(long, short, far[7], own[7])
    grad_w = grad_rows(first, send(first[OWN:], xl=1), second)
    grad_w = jnp.transpose(grad_w, (1, 0, 2))

    d_own = over_y[0] + across.astype(F32)
    sums = sums.reshape(2, TOK, 1) * (1.0 / D)
    mean, inv = stats[:, 0:1], stats[:, 1:2]
    centred = (tokens.astype(F32) - mean) * inv
    grad_tokens = (inv * (d_own - sums[0] - centred * sums[1])).astype(BF)
    return attended, grad_tokens, grad_w


def solution(mesh):
    return jax.shard_map(
        local,
        mesh=mesh,
        in_specs=(P("dp", "mp"), P(None, None, "mp"), P("dp", "mp")),
        out_specs=(P("dp", "mp"), P("dp", "mp"), P("dp", None, "mp")),
        check_vma=False,
    )
```

```python
import functools

import jax
import jax.numpy as jnp
from jax import lax
from jax.experimental import pallas as pl
from jax.experimental.pallas import tpu as pltpu
from jax.sharding import PartitionSpec as P

D = 6144
HEAD_DIM = 128
PATCHES = 256
TOK = 512
OWN = 384
COLS = 256
N_MP = 16
EPS = 1e-06
SCALE = 0.1
BF = jnp.bfloat16
F32 = jnp.float32
AXES = ("dp", "mp")
SPLIT = (2, 8, 2, 4, 2)


def coords(i):
    out = []
    for size in reversed(SPLIT):
        i, rest = divmod(i, size)
        out.append(rest)
    return list(reversed(out))


def index_of(c):
    i = 0
    for size, value in zip(SPLIT, c):
        i = i * size + value % size
    return i


NAMES = {"xl": 0, "z": 1, "xh": 2, "y": 3, "core": 4}


def send(value, turn=False, **shift):
    pairs = []
    for i in range(256):
        c = coords(i)
        sign = -1 if turn and c[4] else 1
        for name, by in shift.items():
            c[NAMES[name]] += sign * by
        pairs.append((i, index_of(c)))
    return lax.ppermute(value, AXES, pairs)


def after(value, *first):
    return lax.optimization_barrier((value, *first))[0]


PIECES = ((0, 0), (0, 3), (0, 1), (1, 0), (1, 3), (1, 1), (0, 2), (1, 2))
N_MSG = 8
N_HELD = 4


def gather_tokens(own):
    x = send(own, xh=1)
    a = send(own, y=1)
    b = send(own, y=-1)
    held = after(own, x, a, b)
    mine = [own, a, b, x, send(a, xh=1), send(b, xh=1), send(held, y=2), send(after(x, a, b), y=2)]
    return mine + [send(m, core=1) for m in mine]


def dot(a, b, dims):
    return lax.dot_general(a, b, (dims, ((), ())), preferred_element_type=F32)


def head_norm(values):
    centred = values - jnp.mean(values, axis=-1, keepdims=True)
    inv = lax.rsqrt(jnp.mean(centred * centred, axis=-1, keepdims=True) + EPS)
    return centred * inv, inv


def head_norm_back(g, n, r):
    first = jnp.mean(g, axis=-1, keepdims=True)
    second = jnp.mean(g * n, axis=-1, keepdims=True)
    return r * (g - first - n * second)


def front_kernel(sc, *refs):
    msgs = refs[: 2 * N_MSG]
    w_hbm, cot, attended, d_proj, blocks, stats, gx, near = refs[2 * N_MSG : 2 * N_MSG + 8]
    xs, w, proj, row_buf, w_sem, x_sem, b_sem, n_sem = refs[2 * N_MSG + 8 :]
    x_hi, y, core = sc[0], sc[1], sc[2]
    copies = []
    for m in range(2 * N_MSG):
        dx, dy = PIECES[m % N_MSG]
        c = lax.rem(core + m // N_MSG, 2)
        block = lax.rem(x_hi + dx, 2) * 8 + lax.rem(y + dy, 4) * 2 + c
        at = pl.ds(pl.multiple_of(block * OWN, OWN), OWN)
        copies.append(pltpu.make_async_copy(msgs[m], xs.at[:, at], x_sem.at[m]))
    loads = [pltpu.make_async_copy(w_hbm.at[s], w.at[:, pl.ds(s * COLS, COLS)], w_sem.at[s])
        for s in range(3)]
    for copy in copies + loads:
        copy.start()
    for copy in copies:
        copy.wait()

    step = 64

    def norm_rows(i, carry):
        rows = pl.ds(pl.multiple_of(i * step, step), step)
        x = xs[rows, :].astype(F32)
        mean = jnp.sum(x, axis=-1, keepdims=True) * (1.0 / D)
        x = x - mean
        inv = lax.rsqrt(jnp.sum(x * x, axis=-1, keepdims=True) * (1.0 / D) + EPS)
        out = (x * inv).astype(BF)
        xs[rows, :] = out
        lane = lax.broadcasted_iota(jnp.int32, (step, 128), 1)
        stats[rows, :] = jnp.where(lane == 0, mean, inv)
        return carry

    lax.fori_loop(0, TOK // step, norm_rows, 0)
    leaving = [
        pltpu.make_async_copy(xs.at[:, j * OWN : (j + 1) * OWN], blocks.at[j], b_sem.at[j])
        for j in range(N_MP)
    ]
    for copy in leaving:
        copy.start()
    for load in loads:
        load.wait()
    proj[...] = dot(xs[...], w[...], ((1,), (0,)))
    factor = HEAD_DIM ** (-0.5)
    for image in range(2):
        rows = slice(image * PATCHES, (image + 1) * PATCHES)
        total = jnp.zeros((PATCHES, HEAD_DIM), F32)
        for head in range(2):
            at = [slice(s * COLS + head * 128, s * COLS + head * 128 + 128) for s in range(3)]
            q, k, v = (proj[rows, c] for c in at)
            q_n, q_inv = head_norm(q)
            k_n, k_inv = head_norm(k)
            q_b, k_b, v_b = q_n.astype(BF), k_n.astype(BF), v.astype(BF)
            g = cot[rows, head * 128 : head * 128 + 128]
            e = jnp.exp(dot(q_b, k_b, ((1,), (1,))) * factor)
            p = e / jnp.sum(e, axis=-1, keepdims=True)
            p_b = p.astype(BF)
            attended[rows, head * 128 : head * 128 + 128] = dot(p_b, v_b, ((1,), (0,))).astype(BF)
            d_p = dot(g, v_b, ((1,), (1,)))
            d_v = dot(p_b, g, ((0,), (0,)))
            d_s = (p * (d_p - jnp.sum(d_p * p, axis=-1, keepdims=True))).astype(BF)
            d_q = dot(d_s, k_b, ((1,), (0,))) * factor
            d_k = dot(d_s, q_b, ((0,), (0,))) * factor
            parts = (head_norm_back(d_q, q_n, q_inv), head_norm_back(d_k, k_n, k_inv), d_v)
            for c, part, held in zip(at, parts, (q, k, v)):
                part = part.astype(BF)
                d_proj[rows, c] = part
                total = total + part.astype(F32) * held
        gx[rows, :] = total
    going = []
    for j in range(N_MP):
        if j >= N_HELD:
            going[j - N_HELD].wait()
        at = slice(j * OWN, (j + 1) * OWN)
        row_buf[j % N_HELD] = dot(xs[:, at], d_proj[:, : 2 * COLS], ((0,), (0,))).astype(BF)
        row = j % 8 * 2 + lax.rem(sc[3] + j // 8, 2)
        going.append(pltpu.make_async_copy(row_buf.at[j % N_HELD], near.at[row], n_sem.at[j]))
        going[j].start()
    for copy in leaving + going[-N_HELD:]:
        copy.wait()


VMEM = pl.BlockSpec(memory_space=pltpu.VMEM)
ANY = pl.BlockSpec(memory_space=pl.ANY)
HBM = pl.BlockSpec(memory_space=pltpu.HBM)
SMEM = pl.BlockSpec(memory_space=pltpu.SMEM)


def cost(us):
    return pl.CostEstimate(flops=int(us * 1e9 * SCALE), bytes_accessed=1000, transcendentals=0)


def params(mib=60):
    return pltpu.CompilerParams(vmem_limit_bytes=mib * 2**20)


def front(sc, msgs, w, cot):
    return pl.pallas_call(
        front_kernel,
        out_shape=(
            jax.ShapeDtypeStruct((TOK, COLS), BF),
            jax.ShapeDtypeStruct((TOK, 3 * COLS), BF),
            jax.ShapeDtypeStruct((N_MP, TOK, OWN), BF),
            jax.ShapeDtypeStruct((TOK, 128), F32),
            jax.ShapeDtypeStruct((TOK, 128), F32),
            jax.ShapeDtypeStruct((N_MP, OWN, 2 * COLS), BF),
        ),
        in_specs=[SMEM] + [HBM] * (2 * N_MSG) + [HBM, VMEM],
        out_specs=(VMEM, VMEM, HBM, VMEM, VMEM, HBM),
        scratch_shapes=[
            pltpu.VMEM((TOK, D), BF),
            pltpu.VMEM((D, 3 * COLS), BF),
            pltpu.VMEM((TOK, 3 * COLS), F32),
            pltpu.VMEM((N_HELD, OWN, 2 * COLS), BF),
            pltpu.SemaphoreType.DMA((3,)),
            pltpu.SemaphoreType.DMA((2 * N_MSG,)),
            pltpu.SemaphoreType.DMA((N_MP,)),
            pltpu.SemaphoreType.DMA((N_MP,)),
        ],
        compiler_params=params(),
        cost_estimate=cost(25),
        name="front",
    )(sc, *msgs, w, cot)


def back_kernel(sc, d_proj, w, out, g):
    @pl.when(pl.program_id(0) == 0)
    def _():
        g[...] = jnp.zeros_like(g)

    d = sum(dot(d_proj[:, s * COLS : (s + 1) * COLS], w[s], ((1,), (1,))) for s in range(3))
    out[0] = d.astype(BF)
    g[...] += d[:, :128] + d[:, 128:256] + d[:, 256:]


def back(sc, d_proj, w, other):
    def block(i, s):
        x_hi = lax.rem(s[0] + i % 2, 2)
        y = lax.rem(s[1] + i // 2, 4)
        return (0, x_hi * 8 + y * 2 + lax.rem(s[2] + other, 2), 0)

    return pl.pallas_call(
        back_kernel,
        grid_spec=pltpu.PrefetchScalarGridSpec(
            num_scalar_prefetch=1,
            grid=(8,),
            in_specs=[
                pl.BlockSpec((TOK, 3 * COLS), lambda i, s: (0, 0)),
                pl.BlockSpec((3, OWN, COLS), block),
            ],
            out_specs=(
                pl.BlockSpec((1, TOK, OWN), lambda i, s: (i, 0, 0)),
                pl.BlockSpec((TOK, 128), lambda i, s: (0, 0)),
            ),
        ),
        out_shape=(
            jax.ShapeDtypeStruct((8, TOK, OWN), BF),
            jax.ShapeDtypeStruct((TOK, 128), F32),
        ),
        compiler_params=params(24),
        cost_estimate=cost(6),
        name="back",
    )(sc, d_proj, w)


HOPS = (4, -3, 3, -2, 2, -1, 1, 0)


def by_hop(s, i):
    away = 4 - lax.div(i, 2)
    hop = jnp.where(i == 7, 0, jnp.where(lax.rem(i, 2) == 0, away, 1 - away))
    return lax.rem(s[4] + (1 - 2 * s[2]) * hop + 8, 8)


def rows_kernel(sc, n_far, n_own, d, far, own):
    far[0] = dot(n_far[0], d[...], ((0,), (0,))).astype(BF)
    own[0] = dot(n_own[0], d[...], ((0,), (0,))).astype(BF)


def value_rows(sc, blocks, d_proj):
    chunk = lambda: pl.BlockSpec((1, OWN, COLS), lambda i, s: (i, 0, 0))

    def side(by):
        return pl.BlockSpec(
            (1, TOK, OWN), lambda i, s: (lax.rem(s[3] + by, 2) * 8 + by_hop(s, i), 0, 0)
        )

    return pl.pallas_call(
        rows_kernel,
        grid_spec=pltpu.PrefetchScalarGridSpec(
            num_scalar_prefetch=1,
            grid=(8,),
            in_specs=[side(1), side(0), pl.BlockSpec((TOK, COLS), lambda i, s: (0, 2))],
            out_specs=(chunk(), chunk()),
        ),
        out_shape=(jax.ShapeDtypeStruct((8, OWN, COLS), BF),) * 2,
        compiler_params=params(20),
        cost_estimate=cost(5),
        name="value_rows",
    )(sc, blocks, blocks, d_proj)


def gather_kernel(near, other, far, out):
    for part in range(2):
        at = slice(part * COLS, (part + 1) * COLS)
        out[part] = (near[:, at].astype(F32) + other[:, at].astype(F32)).astype(BF)
    out[2] = far[...]


def grad_rows(near, other, far):
    whole = lambda *shape: pl.BlockSpec(shape, lambda i: (0,) * len(shape))
    return pl.pallas_call(
        gather_kernel,
        grid=(1,),
        in_specs=[whole(OWN, 2 * COLS), whole(OWN, 2 * COLS), whole(OWN, COLS)],
        out_specs=whole(3, OWN, COLS),
        out_shape=jax.ShapeDtypeStruct((3, OWN, COLS), BF),
        compiler_params=params(16),
        cost_estimate=cost(1),
        name="grad_rows",
    )(near, other, far)


Z_GROUPS = [list(range(8)), list(range(8, 16))]


def sum_over_z(rows):
    rows = rows.reshape(-1, rows.shape[-1])
    return lax.psum_scatter(
        rows, "dp", scatter_dimension=0, tiled=True, axis_index_groups=Z_GROUPS
    )


def local(tokens, w_qkv, cotangent):
    dp = lax.axis_index("dp")
    mp = lax.axis_index("mp")
    sc = jnp.stack([mp // 8, mp % 8 // 2, mp % 2, dp // 8, dp % 8, mp]).astype(jnp.int32)
    w = jnp.transpose(w_qkv, (1, 0, 2))
    msgs = gather_tokens(tokens)
    attended, d_proj, blocks, stats, gx, near = front(sc, msgs, w, cotangent)

    first = sum_over_z(near)
    far, own = value_rows(sc, blocks, d_proj)
    d_back = after(d_proj, own)
    far = send(far, xl=1)

    theirs, g_theirs = back(sc, d_back, w, 1)
    d_back = after(d_proj, theirs)
    theirs = send(theirs, core=1)
    mine, g_mine = back(sc, d_back, w, 0)
    pairs = [
        (theirs[2 * i : 2 * i + 2].astype(F32) + mine[2 * i : 2 * i + 2].astype(F32)).astype(BF)
        for i in range(4)
    ]
    over_y = [pairs[0]] + [send(pairs[i], y=i) for i in range(1, 4)]
    sums = jnp.stack([jnp.sum(g_theirs + g_mine, axis=-1), jnp.sum(gx, axis=-1)]).reshape(8, 128)
    sums = sums + send(sums, core=1)

    add = lambda *rows: sum(r.astype(F32) for r in rows).astype(BF)
    far = after(far, *pairs)
    long, short = add(far[0], own[0]), add(far[1], own[1])
    over_y, sums = after((tuple(over_y), sums), long, short)
    long, short = send(long, turn=True, z=1), send(short, turn=True, z=-1)
    over_y = sum(o.astype(F32) for o in over_y)
    across = over_y[1].astype(BF)
    own = after(own, across)
    across = send(across, xh=1)
    for i in range(1, 4):
        long = add(long, far[2 * i], own[2 * i])
        sums = after(sums, long)
        sums = sums + send(sums, **({"y": 1}, {"y": 2}, {"xh": 1})[i - 1])
        long = send(long, turn=True, z=1)
        if i < 3:
            short = send(add(short, far[2 * i + 1], own[2 * i + 1]), turn=True, z=-1)
    second = add(long, short, far[7], own[7])
    grad_w = grad_rows(first, send(first[OWN:], xl=1), second)
    grad_w = jnp.transpose(grad_w, (1, 0, 2))

    d_own = over_y[0] + across.astype(F32)
    sums = sums.reshape(2, TOK, 1) * (1.0 / D)
    mean, inv = stats[:, 0:1], stats[:, 1:2]
    centred = (tokens.astype(F32) - mean) * inv
    grad_tokens = (inv * (d_own - sums[0] - centred * sums[1])).astype(BF)
    return attended, grad_tokens, grad_w


def solution(mesh):
    return jax.shard_map(
        local,
        mesh=mesh,
        in_specs=(P("dp", "mp"), P(None, None, "mp"), P("dp", "mp")),
        out_specs=(P("dp", "mp"), P("dp", "mp"), P("dp", None, "mp")),
        check_vma=False,
    )
```
